128 devices in a mesh: leaf: 8 (over x, core), top: 16 (over z, y).
Axes of the slice: x: 4, y: 4, z: 4, core: 2. Of those that a mesh axis runs over, the one named last changes fastest.
Arguments:
- points: float32 [3, 2621440], P(None, ('leaf', 'top')), may hold values from 0 to 2561, as said below
- vectors: float32 [8, 2621440], P(None, ('leaf', 'top')), may hold values from -6 to 6
- near_offset: int32 [5120, 2], P(('leaf', 'top')), may hold values from -2 to 2, as said below
- leaf_basis: float32 [5120, 512, 128], P(('leaf', 'top')), may hold values from -0.25 to 0.25
- leaf_transfer: float32 [5120, 128, 128], P(('leaf', 'top')), may hold values from -0.5 to 0.5
- far_target: int32 [128, 16, 8], P(('leaf', 'top')), may hold values from 0 to 40, as said below
- far_source: int32 [128, 16, 8], P(('leaf', 'top')), may hold values from 0 to 39
- far_coupling: float32 [128, 16, 8, 128, 128], P(('leaf', 'top')), may hold values from -0.5 to 0.5
- upper_transfer: float32 [12, 128, 128], replicated, may hold values from -0.375 to 0.375
- upper_coupling: float32 [14, 128, 128], replicated, may hold values from -0.01953125 to 0.01953125
Outputs:
- product: float32 [8, 2621440], P(None, ('leaf', 'top'))
The draws below stay inside these ranges and needn't reach their ends.
Inputs may be any that keep to these rules, and one draw needn't show every extreme that they name: Coordinate 0 of the points of leaf g lies in [g / 2, g / 2 + 1], coordinates 1 and 2 in [0, 1]. `near_offset`: 0 marks an empty slot; the nonzero offsets of a leaf are distinct and lead to a leaf of the grid. `far_target`: 40 marks an empty slot; several slots may name the same target.
All inputs are finite; a program needn't handle non-finite values.
Results may differ from the reference program's by a relative error of at most 0.0003.
Values sent between devices are 32-bit elements; how exact they have to be, the bound alone decides.
No kernel may reach another device: no remote copies, remote signals or barrier semaphores. Data moves between devices by JAX's collectives and lax.ppermute only.
A program may use at most 128 MiB of HBM per device.

```python
import math
import jax
import jax.numpy as jnp
from jax import lax

LEAF = 512
RANK = 128
NRHS = 8
NEAR = 2
CAP = 8
L0_DEV = 40
DEV_COUNT = 128
LEAVES = 5120
NPTS = 2621440
REGION_LEAVES = 640
UP_TRANSFERS = 12
UP_COUPLINGS = 14
N_LEAF = 8
N_TOP = 16


def draw_points(key, part):
    key = jax.random.fold_in(key, 11)
    key_along, key_across = jax.random.split(key)
    owner_leaf_index = (jnp.arange(NPTS, dtype=jnp.int32) // LEAF).astype(jnp.float32)
    along = owner_leaf_index * 0.5 + jax.random.uniform(key_along, (NPTS,), jnp.float32)
    across = jax.random.uniform(key_across, (2, NPTS), jnp.float32)
    return jnp.concatenate([along[None, :], across], axis=0)


def draw_near_offset(key, part):
    key = jax.random.fold_in(key, 12)
    key_order, key_keep = jax.random.split(key)
    scores = jax.random.randint(key_order, (LEAVES, 4), 0, 1048576) * 4 + jnp.arange(4, dtype=jnp.int32)[None, :]
    ordering = jnp.argsort(scores, axis=1)
    candidates = jnp.array([-2, -1, 1, 2], jnp.int32)
    chosen = candidates[ordering[:, :NEAR]]
    keeping = jax.random.randint(key_keep, (LEAVES, NEAR), 0, 4) > 0
    landing = jnp.arange(LEAVES, dtype=jnp.int32)[:, None] + chosen
    inside = (landing >= 0) & (landing < LEAVES)
    return jnp.where(keeping & inside, chosen, 0).astype(jnp.int32)


def draw_far_target(key, part):
    key = jax.random.fold_in(key, 21)
    key_peer, key_used, key_leaf = jax.random.split(key, 3)
    layout = (N_LEAF * N_TOP, N_TOP, CAP)
    full_peer = jax.random.randint(key_peer, (N_LEAF * N_TOP, 1, 1), 0, N_TOP)
    peer_ids = jnp.arange(N_TOP, dtype=jnp.int32)[None, :, None]
    in_use = (jax.random.randint(key_used, layout, 0, 5) < 3) | (peer_ids == full_peer)
    chosen = jax.random.randint(key_leaf, layout, 0, L0_DEV)
    return jnp.where(in_use, chosen, L0_DEV).astype(jnp.int32)


def draw_far_source(key, part):
    key = jax.random.fold_in(key, 31)
    return jax.random.randint(key, (N_LEAF * N_TOP, N_TOP, CAP), 0, L0_DEV).astype(jnp.int32)


def block_levels(stream_key, shape, cuts, smallest, largest):
    factor_of, own = 1.0, jax.random.fold_in(stream_key, 6)
    for position, blocks in cuts:
        heights = jnp.exp(jax.random.uniform(jax.random.fold_in(own, position), (blocks,), jnp.float32, smallest / len(cuts), largest / len(cuts)))
        factor_of = factor_of * jnp.repeat(heights, shape[position] // blocks).reshape([-1 if axis == position else 1 for axis in range(len(shape))])
    return factor_of


def scatter_about(rng, shape, scale, limit, pieces=(), kind=jnp.bfloat16):
    level = block_levels(rng, shape, pieces, -0.22, 0.18) if pieces else 1.0
    values = jax.random.normal(rng, shape, jnp.float32) * scale * level
    return jnp.minimum(jnp.maximum(values, -limit), limit).astype(kind)


def setup_inputs(seed: int = 0) -> dict:
    key_list = jax.random.split(jax.random.key(seed), 11)
    return {
        "points": draw_points(jax.random.fold_in(key_list[10], 71), 0),
        "vectors": scatter_about(key_list[1], (NRHS, NPTS), 1.0, 6.0, ((1, 128),), jnp.float32),
        "near_offset": draw_near_offset(jax.random.fold_in(key_list[10], 71), 0),
        "leaf_basis": scatter_about(key_list[3], (LEAVES, LEAF, RANK), LEAF ** -0.5, 0.25, ((0, 128),), jnp.float32),
        "leaf_transfer": scatter_about(key_list[4], (LEAVES, RANK, RANK), RANK ** -0.5, 0.5, ((0, 128),), jnp.float32),
        "far_target": draw_far_target(jax.random.fold_in(key_list[10], 71), 0),
        "far_source": draw_far_source(jax.random.fold_in(key_list[10], 71), 0),
        "far_coupling": scatter_about(key_list[7], (DEV_COUNT, N_TOP, CAP, RANK, RANK), RANK ** -0.5, 0.5, ((0, 128),), jnp.float32),
        "upper_transfer": scatter_about(key_list[8], (UP_TRANSFERS, RANK, RANK), (2 * RANK) ** -0.5, 0.375, (), jnp.float32),
        "upper_coupling": scatter_about(key_list[9], (UP_COUPLINGS, RANK, RANK), (RANK * REGION_LEAVES) ** -0.5, 0.01953125, (), jnp.float32),
    }


AMPLITUDE = 0.25
NUGGET = 0.1
SCALES = (0.3, 0.15, 0.15)
ROOT_THREE = math.sqrt(3.0)
TOPMOST_LEVEL = lax.Precision.HIGHEST
per_turn = 4

def matern(dist_sq):
    radius = jnp.sqrt(dist_sq)
    return AMPLITUDE * (1.0 + ROOT_THREE * radius) * jnp.exp(-ROOT_THREE * radius)

def nearfield_group(target_pts, target_vec, source_pts, source_vec, weights):
    dist_sq = None
    for axis_index in range(3):
        spread = (target_pts[axis_index][:, None, :, None] - source_pts[axis_index][:, :, None, :]) / SCALES[axis_index]
        dist_sq = spread * spread if dist_sq is None else dist_sq + spread * spread
    kernel = matern(dist_sq) * weights[:, :, None, None]
    result = jnp.einsum('gkts,dgks->dgt', kernel, source_vec, precision=TOPMOST_LEVEL)
    return result + NUGGET * target_vec

def near_all(points, vectors, near_offset):
    columns = vectors.shape[0]
    joined = jnp.concatenate([points, vectors], axis=0)
    padded = jnp.pad(joined, ((0, 0), (2 * LEAF, 2 * LEAF)))
    blocks = padded.reshape(3 + columns, LEAVES + 4, LEAF)
    offsets = jnp.concatenate([jnp.zeros((LEAVES, 1), jnp.int32), near_offset], axis=1)
    weights = jnp.concatenate([jnp.ones((LEAVES, 1), jnp.float32), (near_offset != 0).astype(jnp.float32)], axis=1)
    sources = jnp.arange(LEAVES, dtype=jnp.int32)[:, None] + 2 + offsets

    def one_turn(first_leaf):
        selected_entries = lax.dynamic_slice_in_dim(sources, first_leaf, per_turn, 0)
        mask_rows = lax.dynamic_slice_in_dim(weights, first_leaf, per_turn, 0)
        gathered = jnp.take(blocks, selected_entries, axis=1)
        own_block = lax.dynamic_slice_in_dim(blocks, first_leaf + 2, per_turn, 1)
        return nearfield_group(own_block[:3], own_block[3:], gathered[:3], gathered[3:], mask_rows)
    starts = jnp.arange(LEAVES // per_turn, dtype=jnp.int32) * per_turn
    fields = lax.map(one_turn, starts)
    return jnp.transpose(fields, (1, 0, 2, 3)).reshape(columns, LEAVES * LEAF)

def upper_tree(region_all, upper_transfer, upper_coupling, regions):
    tree_depth = regions.bit_length() - 1
    coeffs = [region_all]
    current = region_all
    for height in range(tree_depth - 1):
        offset = 2 * regions - 2 * (regions >> height)
        node_count = regions >> height
        carried = jnp.einsum('nds,nsq->ndq', current, upper_transfer[offset:offset + node_count], precision=TOPMOST_LEVEL)
        current = carried[0::2] + carried[1::2]
        coeffs.append(current)
    local_exp = None
    for height in reversed(range(tree_depth)):
        offset = 2 * regions - 2 * (regions >> height)
        node_count = regions >> height
        self_coefficient = coeffs[height]
        swapped = jnp.stack([self_coefficient[1::2], self_coefficient[0::2]], axis=1).reshape(self_coefficient.shape)
        at_height = jnp.einsum('nds,nsq->ndq', swapped, upper_coupling[offset:offset + node_count], precision=TOPMOST_LEVEL)
        if local_exp is not None:
            parents = jnp.repeat(local_exp, 2, axis=0)
            at_height = at_height + jnp.einsum('nds,nqs->ndq', parents, upper_transfer[offset:offset + node_count], precision=TOPMOST_LEVEL)
        local_exp = at_height
    return local_exp

def reference(points, vectors, near_offset, leaf_basis, leaf_transfer, far_target, far_source, far_coupling, upper_transfer, upper_coupling):
    columns = vectors.shape[0]
    nearby = near_all(points, vectors, near_offset)
    leaf_coefs = jnp.einsum('dlp,lpr->ldr', vectors.reshape(columns, LEAVES, LEAF), leaf_basis, precision=TOPMOST_LEVEL)
    grouped_coefs = leaf_coefs.reshape(N_LEAF, REGION_LEAVES, columns, RANK)
    grouped_transfer = leaf_transfer.reshape(N_LEAF, REGION_LEAVES, RANK, RANK)
    region_coef = jnp.einsum('nkdr,nkrs->nds', grouped_coefs, grouped_transfer, precision=TOPMOST_LEVEL)
    region_local = upper_tree(region_coef, upper_transfer, upper_coupling, N_LEAF)
    from_above = jnp.einsum('nds,nkqs->nkdq', region_local, grouped_transfer, precision=TOPMOST_LEVEL).reshape(LEAVES, columns, RANK)
    device_ids = jnp.arange(N_LEAF * N_TOP, dtype=jnp.int32)
    region_ids = device_ids // N_TOP
    peer_ids = jnp.arange(N_TOP, dtype=jnp.int32)
    source_ids = (region_ids[:, None, None] * N_TOP + peer_ids[None, :, None]) * L0_DEV + far_source
    selected_entries = jnp.take(leaf_coefs, source_ids.reshape(-1), axis=0)
    kernel_products = jnp.einsum('sdr,srq->sdq', selected_entries, far_coupling.reshape(-1, RANK, RANK), precision=TOPMOST_LEVEL)
    target_ids = jnp.where(far_target < L0_DEV, device_ids[:, None, None] * L0_DEV + far_target, LEAVES)
    far_local = jax.ops.segment_sum(kernel_products, target_ids.reshape(-1).astype(jnp.int32), num_segments=LEAVES + 1)[:LEAVES]
    leaf_local = far_local + from_above
    spread_back = jnp.einsum('ldr,lpr->dlp', leaf_local, leaf_basis, precision=TOPMOST_LEVEL)
    return nearby + spread_back.reshape(columns, LEAVES * LEAF)
```

```python
import functools
import math

import jax
import jax.numpy as jnp
from jax import lax
from jax.experimental import pallas as pl
from jax.experimental.pallas import tpu as pltpu
from jax.sharding import PartitionSpec as P

F32, BF16 = jnp.float32, jnp.bfloat16
NUGGET = 0.1
SCALES = (0.3, 0.15, 0.15)
LOG2E = math.log2(math.e)
FACTOR = tuple(math.sqrt(3.0) * LOG2E / scale for scale in SCALES)
GAIN = -0.25 * math.log(2.0) * math.e
TINY = 1e-20
DEPTH = 64
HALO = 2
VMEM_LIMIT = 48 << 20


def halves(x):
    high = x.astype(BF16)
    return high, (x - high.astype(F32)).astype(BF16)


def thirds(x):
    high = x.astype(BF16).astype(F32)
    rest = x - high
    middle = rest.astype(BF16).astype(F32)
    return high, middle, rest - middle


def dot3(x, matrix, dims):
    x_high, x_low = halves(x)
    m_high, m_low = halves(matrix)
    both = lax.dot_general(
        jnp.concatenate([x_high, x_low], axis=0), m_high, (dims, ((), ())), preferred_element_type=F32
    )
    low = lax.dot_general(
        jnp.concatenate([x_high, jnp.zeros_like(x_high)], axis=0), m_low, (dims, ((), ())), preferred_element_type=F32
    )
    return both[0:8] + both[8:16] + low[0:8]


PLAIN, TURNED = ((1,), (0,)), ((1,), (1,))


def coef_kernel(vec_ref, basis_ref, transfer_ref, coef_ref, sum_ref, *, per_step, leaf_size):
    @pl.when(pl.program_id(0) == 0)
    def _():
        sum_ref[...] = jnp.zeros_like(sum_ref)

    total = jnp.zeros(sum_ref.shape, F32)
    for i in range(per_step):
        coef = dot3(vec_ref[:, i * leaf_size : (i + 1) * leaf_size], basis_ref[i], PLAIN)
        coef_ref[i] = coef
        total += dot3(coef, transfer_ref[i], PLAIN)
    sum_ref[...] += total


def coefficients(vectors, leaf_basis, leaf_transfer):
    leaves, leaf_size, rank = leaf_basis.shape
    columns = vectors.shape[0]
    per_step = 5
    return pl.pallas_call(
        functools.partial(coef_kernel, per_step=per_step, leaf_size=leaf_size),
        grid=(leaves // per_step,),
        in_specs=[
            pl.BlockSpec((columns, per_step * leaf_size), lambda i: (0, i)),
            pl.BlockSpec((per_step, leaf_size, rank), lambda i: (i, 0, 0)),
            pl.BlockSpec((per_step, rank, rank), lambda i: (i, 0, 0)),
        ],
        out_specs=[
            pl.BlockSpec((per_step, columns, rank), lambda i: (i, 0, 0)),
            pl.BlockSpec((columns, rank), lambda i: (0, 0)),
        ],
        out_shape=[
            jax.ShapeDtypeStruct((leaves, columns, rank), F32),
            jax.ShapeDtypeStruct((columns, rank), F32),
        ],
        compiler_params=pltpu.CompilerParams(vmem_limit_bytes=VMEM_LIMIT),
        cost_estimate=pl.CostEstimate(
            flops=leaves * 16 * rank * (leaf_size + rank) * 4,
            bytes_accessed=4 * leaves * rank * (leaf_size + rank),
            transcendentals=0,
        ),
    )(vectors, leaf_basis, leaf_transfer)


def tree_kernel(place_ref, parts_ref, coef_ref, transfer_ref, coupling_ref, out_ref):
    leaves = coef_ref.shape[0]
    out_ref[0:leaves] = coef_ref[...]
    here = place_ref[0]
    half, quarter = here >> 1, here >> 2

    def up(j):
        return dot3(parts_ref[j], transfer_ref[here ^ j], PLAIN)

    first = up(2) + up(3)
    second = dot3(up(4) + up(5), transfer_ref[8 + (half ^ 2)], PLAIN)
    second += dot3(up(6) + up(7), transfer_ref[8 + (half ^ 3)], PLAIN)
    local = dot3(second, coupling_ref[12 + quarter], PLAIN)
    local = dot3(first, coupling_ref[8 + half], PLAIN) + dot3(local, transfer_ref[8 + half], TURNED)
    local = dot3(parts_ref[1], coupling_ref[here], PLAIN) + dot3(local, transfer_ref[here], TURNED)
    out_ref[leaves] = local


def upper_tree(place, parts, coefs, upper_transfer, upper_coupling):
    leaves, columns, rank = coefs.shape
    whole = pl.BlockSpec(memory_space=pltpu.VMEM)
    return pl.pallas_call(
        tree_kernel,
        in_specs=[pl.BlockSpec(memory_space=pltpu.SMEM)] + [whole] * 4,
        out_specs=whole,
        out_shape=jax.ShapeDtypeStruct((leaves + 1, columns, rank), F32),
        compiler_params=pltpu.CompilerParams(vmem_limit_bytes=VMEM_LIMIT),
    )(place, parts, coefs, upper_transfer, upper_coupling)


def features(x, target):
    row = lax.broadcasted_iota(jnp.int32, x.shape, 0)
    norm = jnp.sum(x * x, axis=0, keepdims=True)
    high, middle, low = thirds(jnp.where(row < 3, x, norm))
    norm_row, one_row, factor = (4, 3, -2.0) if target else (3, 4, 1.0)

    def group(coordinates, norms):
        out = jnp.where(row < 3, coordinates * factor, 0.0)
        if norms is not None:
            out = jnp.where(row == norm_row, norms, jnp.where(row == one_row, 1.0, out))
        return out

    if target:
        groups = [group(high, high), group(middle, middle), group(high, low)]
        groups += [group(low, None), group(middle, None), group(high, None)]
    else:
        groups = [group(high, high), group(middle, middle), group(low, low)]
        groups += [group(high, None), group(high, None), group(middle, None)]
    groups += [jnp.zeros_like(x)] * (DEPTH // 8 - 6)
    return jnp.concatenate(groups, axis=0)


def matern(dist_sq):
    dist_sq = jnp.maximum(dist_sq, TINY)
    nt = -LOG2E - dist_sq * lax.rsqrt(dist_sq)
    return nt * jnp.exp2(nt)


def near_kernel(
    first_ref,
    offset_ref,
    points_ref,
    vectors_ref,
    before_p,
    before_v,
    after_p,
    after_v,
    out_ref,
    wide_scr,
    x_scr,
    a_scr,
    v_scr,
    b0,
    b1,
    u0,
    u1,
    kh0,
    kh1,
    kl0,
    kl1,
    item_g,
    item_h,
    *,
    lo,
    hi,
    leaf_size,
):
    rows = leaf_size // 2
    leaves = offset_ref.shape[0]
    first = first_ref[0]
    row8 = lax.broadcasted_iota(jnp.int32, (8, leaf_size), 0)

    def clear(ref):
        def turn(i, _):
            ref[pl.ds(pl.multiple_of(i * 16, 16), 16)] = jnp.zeros((16, leaf_size), ref.dtype)
            return 0

        lax.fori_loop(0, leaf_size // 16, turn, 0)

    for ref in (u0, u1, kh0, kh1, kl0, kl1):
        clear(ref)
    wide_scr[...] = jnp.zeros_like(wide_scr)

    def prepare(p_ref, v_ref, start, stop, origin):
        def turn(h, _):
            at = pl.ds(pl.multiple_of((h - origin) * leaf_size, leaf_size), leaf_size)
            to = h + HALO - lo
            centre = (first + h).astype(F32) * 0.5 + 0.5
            wide_scr[0:3] = p_ref[:, at]
            shift = jnp.where(row8 == 0, centre, 0.5)
            scale = jnp.where(row8 == 0, FACTOR[0], FACTOR[1])
            x = jnp.where(row8 < 3, (wide_scr[...] - shift) * scale, 0.0)
            x_scr[to] = x
            a_scr[to] = features(x, False).T.astype(BF16)
            v_high, v_low = halves(v_ref[:, at])
            v_scr[to, 0:16] = jnp.concatenate([v_high, v_low], axis=0)
            v_scr[to, 16:32] = jnp.concatenate([v_high, jnp.zeros_like(v_high)], axis=0)
            return 0

        lax.fori_loop(start, stop, turn, 0)

    if lo < HALO:
        prepare(before_p, before_v, -HALO, 0, -HALO)
    prepare(points_ref, vectors_ref, max(lo - HALO, 0), min(hi + HALO, leaves), 0)
    if hi > leaves - HALO:
        prepare(after_p, after_v, leaves, leaves + HALO, leaves)

    def listing(g, n):
        at = pl.ds(pl.multiple_of(g * leaf_size, leaf_size), leaf_size)
        to = pl.ds(pl.multiple_of((g - lo) * leaf_size, leaf_size), leaf_size)
        out_ref[:, to] = NUGGET * vectors_ref[:, at]
        item_g[n] = g - lo
        item_h[n] = g - lo + HALO
        n = n + 1
        for j in range(offset_ref.shape[1]):
            offset = offset_ref[g, j]
            item_g[n] = g - lo
            item_h[n] = g - lo + HALO + offset
            n = n + jnp.where(offset != 0, 1, 0)
        return n

    count = lax.fori_loop(lo, hi, listing, 0)

    def target_features(i, b_scr):
        i = jnp.minimum(i, count - 1)
        g, h = item_g[i], item_h[i]
        apart = (g + HALO - h).astype(F32) * (0.5 * FACTOR[0])
        x = x_scr[g + HALO]
        b_scr[...] = features(jnp.where(row8 == 0, x + apart, x), True).astype(BF16)

    def turn(i, b_now, b_next, u_write, u_read, kh_write, kl_write, kh_read, kl_read):
        h_now = item_h[jnp.minimum(i, count - 1)]
        old = jnp.clip(i - 2, 0, count - 1)
        h_old = item_h[old]
        acc = jnp.zeros((16, leaf_size), F32)
        for c in range(0, leaf_size, rows):
            u_write[c : c + rows] = jnp.dot(a_scr[h_now, c : c + rows], b_now[...], preferred_element_type=F32)
            for r in range(c, c + rows, 16):
                high, low = halves(matern(u_read[r : r + 16]))
                kh_write[r : r + 16] = high
                kl_write[r : r + 16] = low
            acc += jnp.dot(v_scr[h_old, 0:16, c : c + rows], kh_read[c : c + rows], preferred_element_type=F32)
            acc += jnp.dot(v_scr[h_old, 16:32, c : c + rows], kl_read[c : c + rows], preferred_element_type=F32)
        target_features(i + 1, b_next)
        done = (acc[0:8] + acc[8:16]) * jnp.where((i >= 2) & (i < count + 2), GAIN, 0.0)
        at = pl.ds(pl.multiple_of(item_g[old] * leaf_size, leaf_size), leaf_size)
        out_ref[:, at] += done

    target_features(0, b0)

    def two_turns(i, _):
        turn(2 * i, b0, b1, u0, u1, kh0, kl0, kh1, kl1)
        turn(2 * i + 1, b1, b0, u1, u0, kh1, kl1, kh0, kl0)
        return 0

    lax.fori_loop(0, (count + 3) >> 1, two_turns, 0)


def near_field(first, near_offset, points, vectors, before, after, lo, hi):
    leaves, slots = near_offset.shape
    columns = vectors.shape[0]
    leaf_size = vectors.shape[1] // leaves
    count = hi - lo
    smem, vmem = pl.BlockSpec(memory_space=pltpu.SMEM), pl.BlockSpec(memory_space=pltpu.VMEM)
    square = (leaf_size, leaf_size)
    return pl.pallas_call(
        functools.partial(near_kernel, lo=lo, hi=hi, leaf_size=leaf_size),
        in_specs=[smem, smem] + [vmem] * 6,
        out_specs=vmem,
        out_shape=jax.ShapeDtypeStruct((columns, count * leaf_size), F32),
        scratch_shapes=[
            pltpu.VMEM((8, leaf_size), F32),
            pltpu.VMEM((count + 2 * HALO, 8, leaf_size), F32),
            pltpu.VMEM((count + 2 * HALO, leaf_size, DEPTH), BF16),
            pltpu.VMEM((count + 2 * HALO, 32, leaf_size), BF16),
            pltpu.VMEM((DEPTH, leaf_size), BF16),
            pltpu.VMEM((DEPTH, leaf_size), BF16),
            pltpu.VMEM(square, F32),
            pltpu.VMEM(square, F32),
            pltpu.VMEM(square, BF16),
            pltpu.VMEM(square, BF16),
            pltpu.VMEM(square, BF16),
            pltpu.VMEM(square, BF16),
            pltpu.SMEM((count * (slots + 1) + 8,), jnp.int32),
            pltpu.SMEM((count * (slots + 1) + 8,), jnp.int32),
        ],
        compiler_params=pltpu.CompilerParams(vmem_limit_bytes=VMEM_LIMIT),
        cost_estimate=pl.CostEstimate(
            flops=count * 3 * leaf_size * leaf_size * 512,
            bytes_accessed=8 * 11 * leaves * leaf_size,
            transcendentals=count * 6 * leaf_size * leaf_size,
        ),
    )(first, near_offset, points, vectors, before[0], before[1], after[0], after[1])


def far_kernel(
    target_ref, source_ref, coef_ref, coupling_ref, transfer_ref, basis_ref, near_ref, out_ref, local_scr, region_scr, *, peers, per_step
):
    step = pl.program_id(0)
    leaves = local_scr.shape[0] - 1
    leaf_size = basis_ref.shape[1]

    @pl.when(step == 0)
    def _():
        local_scr[...] = jnp.zeros_like(local_scr)
        region = coef_ref[leaves]
        for p in range(1, peers):
            region += coef_ref[p * (leaves + 1) + leaves]
        region_scr[...] = region

    @pl.when(step < peers)
    def _():
        for k in range(source_ref.shape[1]):
            coef = coef_ref[step * (leaves + 1) + source_ref[step, k]]
            local_scr[target_ref[step, k]] += dot3(coef, coupling_ref[0, k], PLAIN)

    @pl.when(step >= peers)
    def _():
        for i in range(per_step):
            local = local_scr[(step - peers) * per_step + i] + dot3(region_scr[...], transfer_ref[i], TURNED)
            at = slice(i * leaf_size, (i + 1) * leaf_size)
            out_ref[:, at] = near_ref[:, at] + dot3(local, basis_ref[i], TURNED)


def far_field(targets, sources, coefs, far_coupling, leaf_transfer, leaf_basis, near):
    peers, slots = sources.shape
    leaves, leaf_size, rank = leaf_basis.shape
    columns = near.shape[0]
    per_step = 5
    smem, vmem = pl.BlockSpec(memory_space=pltpu.SMEM), pl.BlockSpec(memory_space=pltpu.VMEM)

    def late(i):
        return jnp.maximum(i - peers, 0)

    return pl.pallas_call(
        functools.partial(far_kernel, peers=peers, per_step=per_step),
        grid=(peers + leaves // per_step,),
        in_specs=[
            smem,
            smem,
            vmem,
            pl.BlockSpec((1, slots, rank, rank), lambda i: (jnp.minimum(i, peers - 1), 0, 0, 0)),
            pl.BlockSpec((per_step, rank, rank), lambda i: (late(i), 0, 0)),
            pl.BlockSpec((per_step, leaf_size, rank), lambda i: (late(i), 0, 0)),
            pl.BlockSpec((columns, per_step * leaf_size), lambda i: (0, late(i))),
        ],
        out_specs=pl.BlockSpec((columns, per_step * leaf_size), lambda i: (0, late(i))),
        out_shape=jax.ShapeDtypeStruct(near.shape, F32),
        scratch_shapes=[pltpu.VMEM((leaves + 1, columns, rank), F32), pltpu.VMEM((columns, rank), F32)],
        compiler_params=pltpu.CompilerParams(vmem_limit_bytes=VMEM_LIMIT),
    )(targets, sources, coefs, far_coupling, leaf_transfer, leaf_basis, near)


def neighbours(points, vectors, width):
    axes = ("leaf", "top")
    count = lax.axis_size("leaf") * lax.axis_size("top")
    joined = [jnp.concatenate([points[:, s], vectors[:, s]], axis=0) for s in (slice(-width, None), slice(0, width))]
    before = lax.ppermute(joined[0], axes, [(i, i + 1) for i in range(count - 1)])
    after = lax.ppermute(joined[1], axes, [(i + 1, i) for i in range(count - 1)])
    return (before[:3], before[3:]), (after[:3], after[3:])


def shards(
    points,
    vectors,
    near_offset,
    leaf_basis,
    leaf_transfer,
    far_target,
    far_source,
    far_coupling,
    upper_transfer,
    upper_coupling,
):
    leaves, leaf_size, _ = leaf_basis.shape
    regions, peers = lax.axis_size("leaf"), lax.axis_size("top")
    region, peer = lax.axis_index("leaf"), lax.axis_index("top")
    place = region.astype(jnp.int32).reshape(1)
    first = ((region * peers + peer) * leaves).astype(jnp.int32).reshape(1)

    before, after = neighbours(points, vectors, HALO * leaf_size)
    coefs, part = coefficients(vectors, leaf_basis, leaf_transfer)
    parts = [part] + [lax.ppermute(part, "leaf", [(i, i ^ j) for i in range(regions)]) for j in range(1, regions)]
    packed = upper_tree(place, jnp.stack(parts), coefs, upper_transfer, upper_coupling)
    everyone = lax.all_gather(packed, "top", axis=0, tiled=True)
    near = near_field(first, near_offset, points, vectors, before, after, 0, leaves)
    return far_field(far_target[0], far_source[0], everyone, far_coupling[0], leaf_transfer, leaf_basis, near)


def solution(mesh):
    split = ("leaf", "top")
    in_specs = (
        P(None, split),
        P(None, split),
        P(split, None),
        P(split, None, None),
        P(split, None, None),
        P(split, None, None),
        P(split, None, None),
        P(split, None, None, None, None),
        P(),
        P(),
    )
    return jax.shard_map(shards, mesh=mesh, in_specs=in_specs, out_specs=P(None, split), check_vma=False)
```

```python
import functools
import math

import jax
import jax.numpy as jnp
from jax import lax
from jax.experimental import pallas as pl
from jax.experimental.pallas import tpu as pltpu
from jax.sharding import PartitionSpec as P

F32, BF16 = jnp.float32, jnp.bfloat16
NUGGET = 0.1
SCALES = (0.3, 0.15, 0.15)
LOG2E = math.log2(math.e)
FACTOR = tuple(math.sqrt(3.0) * LOG2E / scale for scale in SCALES)
GAIN = -0.25 * math.log(2.0) * math.e
TINY = 1e-20
DEPTH = 64
HALO = 2
VMEM_LIMIT = 48 << 20
WIDE_LIMIT = 56 << 20


def halves(x):
    high = x.astype(BF16)
    return high, (x - high.astype(F32)).astype(BF16)


def thirds(x):
    high = x.astype(BF16).astype(F32)
    rest = x - high
    middle = rest.astype(BF16).astype(F32)
    return high, middle, rest - middle


def dot_plain(x, matrix):
    n = matrix.shape[1]
    left = jnp.concatenate(halves(x), axis=0)
    out = jnp.dot(left, jnp.concatenate(halves(matrix), axis=1), preferred_element_type=F32)
    return out[0:8, 0:n] + out[8:16, 0:n] + out[0:8, n : 2 * n]


def dot_turned(x, matrix):
    high, low = halves(x)
    upper = jnp.concatenate([high, high], axis=1)
    lower = jnp.concatenate([low, jnp.zeros_like(low)], axis=1)
    out = lax.dot_general(
        jnp.concatenate([upper, lower], axis=0),
        jnp.concatenate(halves(matrix), axis=1),
        (((1,), (1,)), ((), ())),
        preferred_element_type=F32,
    )
    return out[0:8] + out[8:16]


def coef_kernel(place_ref, vec_ref, basis_ref, transfer_ref, up0_ref, up1_ref, coef_ref, part_ref, *, per_step, leaf_size):
    del place_ref
    step = pl.program_id(0)

    @pl.when(step == 0)
    def _():
        part_ref[...] = jnp.zeros_like(part_ref)

    total = jnp.zeros(part_ref.shape[1:], F32)
    for i in range(per_step):
        coef = dot_plain(vec_ref[:, i * leaf_size : (i + 1) * leaf_size], basis_ref[i])
        coef_ref[i] = coef
        total += dot_plain(coef, transfer_ref[i])
    part_ref[0] += total

    @pl.when(step == pl.num_programs(0) - 1)
    def _():
        part_ref[1] = dot_plain(part_ref[0], up0_ref[0])
        part_ref[2] = dot_plain(part_ref[1], up1_ref[0])


def coefficients(place, vectors, leaf_basis, leaf_transfer, upper_transfer):
    leaves, leaf_size, rank = leaf_basis.shape
    columns = vectors.shape[0]
    per_step = 5
    node = (1, rank, rank)
    return pl.pallas_call(
        functools.partial(coef_kernel, per_step=per_step, leaf_size=leaf_size),
        grid_spec=pltpu.PrefetchScalarGridSpec(
            num_scalar_prefetch=1,
            grid=(leaves // per_step,),
            in_specs=[
                pl.BlockSpec((columns, per_step * leaf_size), lambda i, p: (0, i)),
                pl.BlockSpec((per_step, leaf_size, rank), lambda i, p: (i, 0, 0)),
                pl.BlockSpec((per_step, rank, rank), lambda i, p: (i, 0, 0)),
                pl.BlockSpec(node, lambda i, p: (p[0], 0, 0)),
                pl.BlockSpec(node, lambda i, p: (8 + (p[0] >> 1), 0, 0)),
            ],
            out_specs=[
                pl.BlockSpec((per_step, columns, rank), lambda i, p: (i, 0, 0)),
                pl.BlockSpec((3, columns, rank), lambda i, p: (0, 0, 0)),
            ],
        ),
        out_shape=[
            jax.ShapeDtypeStruct((leaves, columns, rank), F32),
            jax.ShapeDtypeStruct((3, columns, rank), F32),
        ],
        compiler_params=pltpu.CompilerParams(vmem_limit_bytes=WIDE_LIMIT),
        cost_estimate=pl.CostEstimate(
            flops=leaves * 16 * rank * (leaf_size + rank) * 4,
            bytes_accessed=4 * leaves * rank * (leaf_size + rank),
            transcendentals=0,
        ),
    )(place, vectors, leaf_basis, leaf_transfer, upper_transfer, upper_transfer)


def features(x, target):
    row = lax.broadcasted_iota(jnp.int32, x.shape, 0)
    norm = jnp.sum(x * x, axis=0, keepdims=True)
    high, middle, low = thirds(jnp.where(row < 3, x, norm))
    norm_row, one_row, factor = (4, 3, -2.0) if target else (3, 4, 1.0)

    def group(coordinates, norms):
        out = jnp.where(row < 3, coordinates * factor, 0.0)
        if norms is not None:
            out = jnp.where(row == norm_row, norms, jnp.where(row == one_row, 1.0, out))
        return out

    if target:
        groups = [group(high, high), group(middle, middle), group(high, low)]
        groups += [group(low, None), group(middle, None), group(high, None)]
    else:
        groups = [group(high, high), group(middle, middle), group(low, low)]
        groups += [group(high, None), group(high, None), group(middle, None)]
    groups += [jnp.zeros_like(x)] * (DEPTH // 8 - 6)
    return jnp.concatenate(groups, axis=0)


def matern(dist_sq):
    dist_sq = jnp.maximum(dist_sq, TINY)
    nt = -LOG2E - dist_sq * lax.rsqrt(dist_sq)
    return nt * jnp.exp2(nt)


def near_kernel(
    first_ref,
    offset_ref,
    points_ref,
    vectors_ref,
    before_p,
    before_v,
    after_p,
    after_v,
    out_ref,
    wide_scr,
    x_scr,
    a_scr,
    v_scr,
    b0,
    b1,
    u0,
    u1,
    kh0,
    kh1,
    kl0,
    kl1,
    item_g,
    item_h,
    *,
    lo,
    hi,
    leaf_size,
):
    rows = leaf_size // 2
    leaves = offset_ref.shape[0]
    first = first_ref[0]
    row8 = lax.broadcasted_iota(jnp.int32, (8, leaf_size), 0)

    def clear(ref):
        def turn(i, _):
            ref[pl.ds(pl.multiple_of(i * 16, 16), 16)] = jnp.zeros((16, leaf_size), ref.dtype)
            return 0

        lax.fori_loop(0, leaf_size // 16, turn, 0)

    for ref in (u0, u1, kh0, kh1, kl0, kl1):
        clear(ref)
    wide_scr[...] = jnp.zeros_like(wide_scr)

    def prepare(p_ref, v_ref, start, stop, origin):
        def turn(h, _):
            at = pl.ds(pl.multiple_of((h - origin) * leaf_size, leaf_size), leaf_size)
            to = h + HALO - lo
            centre = (first + h).astype(F32) * 0.5 + 0.5
            wide_scr[0:3] = p_ref[:, at]
            shift = jnp.where(row8 == 0, centre, 0.5)
            scale = jnp.where(row8 == 0, FACTOR[0], FACTOR[1])
            x = jnp.where(row8 < 3, (wide_scr[...] - shift) * scale, 0.0)
            x_scr[to] = x
            a_scr[to] = features(x, False).T.astype(BF16)
            v_high, v_low = halves(v_ref[:, at])
            v_scr[to, 0:16] = jnp.concatenate([v_high, v_low], axis=0)
            v_scr[to, 16:32] = jnp.concatenate([v_high, jnp.zeros_like(v_high)], axis=0)
            return 0

        lax.fori_loop(start, stop, turn, 0)

    if lo < HALO:
        prepare(before_p, before_v, -HALO, 0, -HALO)
    prepare(points_ref, vectors_ref, max(lo - HALO, 0), min(hi + HALO, leaves), 0)
    if hi > leaves - HALO:
        prepare(after_p, after_v, leaves, leaves + HALO, leaves)

    def listing(g, n):
        at = pl.ds(pl.multiple_of(g * leaf_size, leaf_size), leaf_size)
        to = pl.ds(pl.multiple_of((g - lo) * leaf_size, leaf_size), leaf_size)
        out_ref[:, to] = NUGGET * vectors_ref[:, at]
        item_g[n] = g - lo
        item_h[n] = g - lo + HALO
        n = n + 1
        for j in range(offset_ref.shape[1]):
            offset = offset_ref[g, j]
            item_g[n] = g - lo
            item_h[n] = g - lo + HALO + offset
            n = n + jnp.where(offset != 0, 1, 0)
        return n

    count = lax.fori_loop(lo, hi, listing, 0)

    def target_features(i, b_scr):
        i = jnp.minimum(i, count - 1)
        g, h = item_g[i], item_h[i]
        apart = (g + HALO - h).astype(F32) * (0.5 * FACTOR[0])
        x = x_scr[g + HALO]
        b_scr[...] = features(jnp.where(row8 == 0, x + apart, x), True).astype(BF16)

    def turn(i, b_now, b_next, u_write, u_read, kh_write, kl_write, kh_read, kl_read):
        h_now = item_h[jnp.minimum(i, count - 1)]
        old = jnp.clip(i - 2, 0, count - 1)
        h_old = item_h[old]
        acc = jnp.zeros((16, leaf_size), F32)
        for c in range(0, leaf_size, rows):
            u_write[c : c + rows] = jnp.dot(a_scr[h_now, c : c + rows], b_now[...], preferred_element_type=F32)
            for r in range(c, c + rows, 16):
                high, low = halves(matern(u_read[r : r + 16]))
                kh_write[r : r + 16] = high
                kl_write[r : r + 16] = low
            acc += jnp.dot(v_scr[h_old, 0:16, c : c + rows], kh_read[c : c + rows], preferred_element_type=F32)
            acc += jnp.dot(v_scr[h_old, 16:32, c : c + rows], kl_read[c : c + rows], preferred_element_type=F32)
        target_features(i + 1, b_next)
        done = (acc[0:8] + acc[8:16]) * jnp.where((i >= 2) & (i < count + 2), GAIN, 0.0)
        at = pl.ds(pl.multiple_of(item_g[old] * leaf_size, leaf_size), leaf_size)
        out_ref[:, at] += done

    target_features(0, b0)

    def two_turns(i, _):
        turn(2 * i, b0, b1, u0, u1, kh0, kl0, kh1, kl1)
        turn(2 * i + 1, b1, b0, u1, u0, kh1, kl1, kh0, kl0)
        return 0

    lax.fori_loop(0, (count + 3) >> 1, two_turns, 0)


def near_field(first, near_offset, points, vectors, before, after, lo, hi):
    leaves, slots = near_offset.shape
    columns = vectors.shape[0]
    leaf_size = vectors.shape[1] // leaves
    count = hi - lo
    smem, vmem = pl.BlockSpec(memory_space=pltpu.SMEM), pl.BlockSpec(memory_space=pltpu.VMEM)
    square = (leaf_size, leaf_size)
    return pl.pallas_call(
        functools.partial(near_kernel, lo=lo, hi=hi, leaf_size=leaf_size),
        in_specs=[smem, smem] + [vmem] * 6,
        out_specs=vmem,
        out_shape=jax.ShapeDtypeStruct((columns, count * leaf_size), F32),
        scratch_shapes=[
            pltpu.VMEM((8, leaf_size), F32),
            pltpu.VMEM((count + 2 * HALO, 8, leaf_size), F32),
            pltpu.VMEM((count + 2 * HALO, leaf_size, DEPTH), BF16),
            pltpu.VMEM((count + 2 * HALO, 32, leaf_size), BF16),
            pltpu.VMEM((DEPTH, leaf_size), BF16),
            pltpu.VMEM((DEPTH, leaf_size), BF16),
            pltpu.VMEM(square, F32),
            pltpu.VMEM(square, F32),
            pltpu.VMEM(square, BF16),
            pltpu.VMEM(square, BF16),
            pltpu.VMEM(square, BF16),
            pltpu.VMEM(square, BF16),
            pltpu.SMEM((count * (slots + 1) + 8,), jnp.int32),
            pltpu.SMEM((count * (slots + 1) + 8,), jnp.int32),
        ],
        compiler_params=pltpu.CompilerParams(vmem_limit_bytes=VMEM_LIMIT),
        cost_estimate=pl.CostEstimate(
            flops=count * 3 * leaf_size * leaf_size * 512,
            bytes_accessed=8 * 11 * leaves * leaf_size,
            transcendentals=count * 6 * leaf_size * leaf_size,
        ),
    )(first, near_offset, points, vectors, before[0], before[1], after[0], after[1])


def far_kernel(
    place_ref,
    target_ref,
    source_ref,
    parts_ref,
    down0_ref,
    down1_ref,
    across0_ref,
    across1_ref,
    across2_ref,
    coef_ref,
    coupling_ref,
    transfer_ref,
    basis_ref,
    near_ref,
    out_ref,
    local_scr,
    region_scr,
    *,
    far_steps,
    peers,
    per_step,
):
    step = pl.program_id(0)
    leaf_size = basis_ref.shape[1]
    per_far, slots = coupling_ref.shape[0], coupling_ref.shape[1]

    @pl.when(step == 0)
    def _():
        local_scr[...] = jnp.zeros_like(local_scr)
        here = place_ref[0]

        def summed(level):
            first = ((here >> level) ^ 1) << level
            chains = [None] * 4
            for i in range(peers << level):
                part = parts_ref[3 * (first * peers + i) + level]
                chains[i % 4] = part if chains[i % 4] is None else chains[i % 4] + part
            return (chains[0] + chains[1]) + (chains[2] + chains[3])

        local = dot_plain(summed(2), across2_ref[0])
        local = dot_plain(summed(1), across1_ref[0]) + dot_turned(local, down1_ref[0])
        region_scr[...] = dot_plain(summed(0), across0_ref[0]) + dot_turned(local, down0_ref[0])

    @pl.when(step < far_steps)
    def _():
        for p in range(per_far):
            for k in range(slots):
                coef = coef_ref[p, source_ref[step * per_far + p, k]]
                local_scr[target_ref[step * per_far + p, k]] += dot_plain(coef, coupling_ref[p, k])

    @pl.when(step >= far_steps)
    def _():
        for i in range(per_step):
            local = local_scr[(step - far_steps) * per_step + i] + dot_turned(region_scr[...], transfer_ref[i])
            at = slice(i * leaf_size, (i + 1) * leaf_size)
            out_ref[:, at] = near_ref[:, at] + dot_turned(local, basis_ref[i])


def far_field(place, targets, sources, parts, coefs, far_coupling, upper_transfer, upper_coupling, leaf_transfer, leaf_basis, near):
    peers, slots = sources.shape
    leaves, leaf_size, rank = leaf_basis.shape
    columns = near.shape[0]
    per_step, per_far = 5, 2
    far_steps = peers // per_far
    node = (1, rank, rank)

    def soon(i):
        return jnp.minimum(i, far_steps - 1)

    def late(i):
        return jnp.maximum(i - far_steps, 0)

    return pl.pallas_call(
        functools.partial(far_kernel, far_steps=far_steps, peers=peers, per_step=per_step),
        grid_spec=pltpu.PrefetchScalarGridSpec(
            num_scalar_prefetch=3,
            grid=(far_steps + leaves // per_step,),
            in_specs=[
                pl.BlockSpec(parts.shape, lambda i, p, t, s: (0, 0, 0)),
                pl.BlockSpec(node, lambda i, p, t, s: (p[0], 0, 0)),
                pl.BlockSpec(node, lambda i, p, t, s: (8 + (p[0] >> 1), 0, 0)),
                pl.BlockSpec(node, lambda i, p, t, s: (p[0], 0, 0)),
                pl.BlockSpec(node, lambda i, p, t, s: (8 + (p[0] >> 1), 0, 0)),
                pl.BlockSpec(node, lambda i, p, t, s: (12 + (p[0] >> 2), 0, 0)),
                pl.BlockSpec((per_far, leaves, columns, rank), lambda i, p, t, s: (soon(i), 0, 0, 0)),
                pl.BlockSpec((per_far, slots, rank, rank), lambda i, p, t, s: (soon(i), 0, 0, 0)),
                pl.BlockSpec((per_step, rank, rank), lambda i, p, t, s: (late(i), 0, 0)),
                pl.BlockSpec((per_step, leaf_size, rank), lambda i, p, t, s: (late(i), 0, 0)),
                pl.BlockSpec((columns, per_step * leaf_size), lambda i, p, t, s: (0, late(i))),
            ],
            out_specs=pl.BlockSpec((columns, per_step * leaf_size), lambda i, p, t, s: (0, late(i))),
            scratch_shapes=[pltpu.VMEM((leaves + 1, columns, rank), F32), pltpu.VMEM((columns, rank), F32)],
        ),
        out_shape=jax.ShapeDtypeStruct(near.shape, F32),
        compiler_params=pltpu.CompilerParams(vmem_limit_bytes=WIDE_LIMIT),
    )(
        place,
        targets,
        sources,
        parts,
        upper_transfer,
        upper_transfer,
        upper_coupling,
        upper_coupling,
        upper_coupling,
        coefs,
        far_coupling,
        leaf_transfer,
        leaf_basis,
        near,
    )


def neighbours(points, vectors, width):
    axes = ("leaf", "top")
    count = lax.axis_size("leaf") * lax.axis_size("top")
    joined = [jnp.concatenate([points[:, s], vectors[:, s]], axis=0) for s in (slice(-width, None), slice(0, width))]
    before = lax.ppermute(joined[0], axes, [(i, i + 1) for i in range(count - 1)])
    after = lax.ppermute(joined[1], axes, [(i + 1, i) for i in range(count - 1)])
    return (before[:3], before[3:]), (after[:3], after[3:])


def shards(
    points,
    vectors,
    near_offset,
    leaf_basis,
    leaf_transfer,
    far_target,
    far_source,
    far_coupling,
    upper_transfer,
    upper_coupling,
):
    leaves, leaf_size, _ = leaf_basis.shape
    peers = lax.axis_size("top")
    region, peer = lax.axis_index("leaf"), lax.axis_index("top")
    place = region.astype(jnp.int32).reshape(1)
    first = ((region * peers + peer) * leaves).astype(jnp.int32).reshape(1)

    before, after = neighbours(points, vectors, HALO * leaf_size)
    coefs, parts = coefficients(place, vectors, leaf_basis, leaf_transfer, upper_transfer)
    all_parts = lax.all_gather(parts, ("leaf", "top"), axis=0, tiled=True)
    all_coefs = lax.all_gather(coefs, "top", axis=0)
    near = near_field(first, near_offset, points, vectors, before, after, 0, leaves)
    return far_field(
        place,
        far_target[0],
        far_source[0],
        all_parts,
        all_coefs,
        far_coupling[0],
        upper_transfer,
        upper_coupling,
        leaf_transfer,
        leaf_basis,
        near,
    )


def solution(mesh):
    split = ("leaf", "top")
    in_specs = (
        P(None, split),
        P(None, split),
        P(split, None),
        P(split, None, None),
        P(split, None, None),
        P(split, None, None),
        P(split, None, None),
        P(split, None, None, None, None),
        P(),
        P(),
    )
    return jax.shard_map(shards, mesh=mesh, in_specs=in_specs, out_specs=P(None, split), check_vma=False)
```

```python
import functools
import math

import jax
import jax.numpy as jnp
from jax import lax
from jax.experimental import pallas as pl
from jax.experimental.pallas import tpu as pltpu
from jax.sharding import PartitionSpec as P

F32, BF16 = jnp.float32, jnp.bfloat16
NUGGET = 0.1
SCALES = (0.3, 0.15, 0.15)
LOG2E = math.log2(math.e)
FACTOR = tuple(math.sqrt(3.0) * LOG2E / scale for scale in SCALES)
GAIN = -0.25 * math.log(2.0) * math.e
TINY = 1e-20
DEPTH = 64
HALO = 2
NEAR_LIMIT = 20 << 20
WIDE_LIMIT = 56 << 20
EARLY_LEAVES = 26


def halves(x):
    high = x.astype(BF16)
    return high, (x - high.astype(F32)).astype(BF16)


def thirds(x):
    high = x.astype(BF16).astype(F32)
    rest = x - high
    middle = rest.astype(BF16).astype(F32)
    return high, middle, rest - middle


def dot_plain(x, matrix):
    n = matrix.shape[1]
    left = jnp.concatenate(halves(x), axis=0)
    out = jnp.dot(left, jnp.concatenate(halves(matrix), axis=1), preferred_element_type=F32)
    return out[0:8, 0:n] + out[8:16, 0:n] + out[0:8, n : 2 * n]


def dot_turned(x, matrix):
    high, low = halves(x)
    upper = jnp.concatenate([high, high], axis=1)
    lower = jnp.concatenate([low, jnp.zeros_like(low)], axis=1)
    out = lax.dot_general(
        jnp.concatenate([upper, lower], axis=0),
        jnp.concatenate(halves(matrix), axis=1),
        (((1,), (1,)), ((), ())),
        preferred_element_type=F32,
    )
    return out[0:8] + out[8:16]


def coef_kernel(place_ref, vec_hbm, basis_hbm, transfer_hbm, up0_ref, up1_ref, coef_ref, part_ref, vec, basis, transfer, sems, *, group):
    del place_ref
    leaves, leaf_size, _ = basis.shape
    groups = leaves // group

    def copies(i):
        at = pl.ds(i * group, group)
        points = pl.ds(pl.multiple_of(i * (group * leaf_size), group * leaf_size), group * leaf_size)
        return (
            pltpu.make_async_copy(vec_hbm.at[:, points], vec.at[:, points], sems.at[0, i]),
            pltpu.make_async_copy(basis_hbm.at[at], basis.at[at], sems.at[1, i]),
            pltpu.make_async_copy(transfer_hbm.at[at], transfer.at[at], sems.at[2, i]),
        )

    for i in range(groups):
        for copy in copies(i):
            copy.start()

    def turn(i, total):
        for copy in copies(i):
            copy.wait()
        coefs = []
        for j in range(group):
            at = pl.ds(pl.multiple_of((i * group + j) * leaf_size, leaf_size), leaf_size)
            coefs.append(dot_plain(vec[:, at], basis[i * group + j]))
        for j in range(group):
            coef_ref[i * group + j] = coefs[j]
            total += dot_plain(coefs[j], transfer[i * group + j])
        return total

    part = lax.fori_loop(0, groups, turn, jnp.zeros(part_ref.shape[1:], F32))
    part_ref[0] = part
    part = dot_plain(part, up0_ref[0])
    part_ref[1] = part
    part_ref[2] = dot_plain(part, up1_ref[0])


def coefficients(place, vectors, leaf_basis, leaf_transfer, upper_transfer):
    leaves, leaf_size, rank = leaf_basis.shape
    columns = vectors.shape[0]
    group = 4
    node = (1, rank, rank)
    hbm = pl.BlockSpec(memory_space=pl.ANY)
    return pl.pallas_call(
        functools.partial(coef_kernel, group=group),
        grid_spec=pltpu.PrefetchScalarGridSpec(
            num_scalar_prefetch=1,
            grid=(1,),
            in_specs=[
                hbm,
                hbm,
                hbm,
                pl.BlockSpec(node, lambda i, p: (p[0], 0, 0)),
                pl.BlockSpec(node, lambda i, p: (8 + (p[0] >> 1), 0, 0)),
            ],
            out_specs=[
                pl.BlockSpec((leaves + 3, columns, rank), lambda i, p: (0, 0, 0)),
                pl.BlockSpec((3, columns, rank), lambda i, p: (0, 0, 0)),
            ],
            scratch_shapes=[
                pltpu.VMEM(vectors.shape, F32),
                pltpu.VMEM(leaf_basis.shape, F32),
                pltpu.VMEM(leaf_transfer.shape, F32),
                pltpu.SemaphoreType.DMA((3, leaves // group)),
            ],
        ),
        out_shape=[
            jax.ShapeDtypeStruct((leaves + 3, columns, rank), F32),
            jax.ShapeDtypeStruct((3, columns, rank), F32),
        ],
        compiler_params=pltpu.CompilerParams(vmem_limit_bytes=WIDE_LIMIT),
        cost_estimate=pl.CostEstimate(
            flops=leaves * 16 * rank * (leaf_size + rank) * 4,
            bytes_accessed=4 * leaves * rank * (leaf_size + rank),
            transcendentals=0,
        ),
    )(place, vectors, leaf_basis, leaf_transfer, upper_transfer, upper_transfer)


def siblings(parts):
    count = lax.axis_size("leaf")

    def from_partner(x, distance):
        return lax.ppermute(x, "leaf", [(i, i ^ distance) for i in range(count)])

    other = from_partner(parts, 1)
    level0, parts = other[0:1], parts[1:] + other[1:]
    other = from_partner(parts, 2)
    level1, parts = other[0:1], parts[1:] + other[1:]
    return level0, level1, from_partner(parts, 4)


def features(x, target):
    row = lax.broadcasted_iota(jnp.int32, x.shape, 0)
    norm = jnp.sum(x * x, axis=0, keepdims=True)
    high, middle, low = thirds(jnp.where(row < 3, x, norm))
    norm_row, one_row, factor = (4, 3, -2.0) if target else (3, 4, 1.0)

    def group(coordinates, norms):
        out = jnp.where(row < 3, coordinates * factor, 0.0)
        if norms is not None:
            out = jnp.where(row == norm_row, norms, jnp.where(row == one_row, 1.0, out))
        return out

    if target:
        groups = [group(high, high), group(middle, middle), group(high, low)]
        groups += [group(low, None), group(middle, None), group(high, None)]
    else:
        groups = [group(high, high), group(middle, middle), group(low, low)]
        groups += [group(high, None), group(high, None), group(middle, None)]
    groups += [jnp.zeros_like(x)] * (DEPTH // 8 - 6)
    return jnp.concatenate(groups, axis=0)


def matern(dist_sq):
    dist_sq = jnp.maximum(dist_sq, TINY)
    nt = -LOG2E - dist_sq * lax.rsqrt(dist_sq)
    return nt * jnp.exp2(nt)


def near_core(inputs, out_ref, scratch, *, lo, hi, base, leaf_size):
    first_ref, offset_ref, points_ref, vectors_ref, before_p, before_v, after_p, after_v = inputs
    wide_scr, x_scr, a_scr, v_scr, b0, b1, u0, u1, kh0, kh1, kl0, kl1, item_g, item_h = scratch
    rows = leaf_size // 2
    leaves = offset_ref.shape[0]
    first = first_ref[0]
    row8 = lax.broadcasted_iota(jnp.int32, (8, leaf_size), 0)

    def clear(ref):
        def turn(i, _):
            ref[pl.ds(pl.multiple_of(i * 16, 16), 16)] = jnp.zeros((16, leaf_size), ref.dtype)
            return 0

        lax.fori_loop(0, leaf_size // 16, turn, 0)

    for ref in (u0, u1, kh0, kh1, kl0, kl1):
        clear(ref)
    wide_scr[...] = jnp.zeros_like(wide_scr)

    def prepare(p_ref, v_ref, start, stop, origin):
        def turn(h, _):
            at = pl.ds(pl.multiple_of((h - origin) * leaf_size, leaf_size), leaf_size)
            to = h + HALO - lo
            centre = (first + h).astype(F32) * 0.5 + 0.5
            wide_scr[0:3] = p_ref[:, at]
            shift = jnp.where(row8 == 0, centre, 0.5)
            scale = jnp.where(row8 == 0, FACTOR[0], FACTOR[1])
            x = jnp.where(row8 < 3, (wide_scr[...] - shift) * scale, 0.0)
            x_scr[to] = x
            a_scr[to] = features(x, False).T.astype(BF16)
            v_high, v_low = halves(v_ref[:, at])
            v_scr[to, 0:16] = jnp.concatenate([v_high, v_low], axis=0)
            v_scr[to, 16:32] = jnp.concatenate([v_high, jnp.zeros_like(v_high)], axis=0)
            return 0

        lax.fori_loop(start, stop, turn, 0)

    if lo < HALO:
        prepare(before_p, before_v, -HALO, 0, -HALO)
    prepare(points_ref, vectors_ref, max(lo - HALO, 0), min(hi + HALO, leaves), 0)
    if hi > leaves - HALO:
        prepare(after_p, after_v, leaves, leaves + HALO, leaves)

    def listing(g, n):
        at = pl.ds(pl.multiple_of(g * leaf_size, leaf_size), leaf_size)
        to = pl.ds(pl.multiple_of((g - base) * leaf_size, leaf_size), leaf_size)
        out_ref[:, to] = NUGGET * vectors_ref[:, at]
        item_g[n] = g - lo
        item_h[n] = g - lo + HALO
        n = n + 1
        for j in range(offset_ref.shape[1]):
            offset = offset_ref[g, j]
            item_g[n] = g - lo
            item_h[n] = g - lo + HALO + offset
            n = n + jnp.where(offset != 0, 1, 0)
        return n

    count = lax.fori_loop(lo, hi, listing, 0)

    def target_features(i, b_scr):
        i = jnp.minimum(i, count - 1)
        g, h = item_g[i], item_h[i]
        apart = (g + HALO - h).astype(F32) * (0.5 * FACTOR[0])
        x = x_scr[g + HALO]
        b_scr[...] = features(jnp.where(row8 == 0, x + apart, x), True).astype(BF16)

    def turn(i, b_now, b_next, u_write, u_read, kh_write, kl_write, kh_read, kl_read):
        h_now = item_h[jnp.minimum(i, count - 1)]
        old = jnp.clip(i - 2, 0, count - 1)
        h_old = item_h[old]
        acc = jnp.zeros((16, leaf_size), F32)
        for c in range(0, leaf_size, rows):
            u_write[c : c + rows] = jnp.dot(a_scr[h_now, c : c + rows], b_now[...], preferred_element_type=F32)
            for r in range(c, c + rows, 16):
                high, low = halves(matern(u_read[r : r + 16]))
                kh_write[r : r + 16] = high
                kl_write[r : r + 16] = low
            acc += jnp.dot(v_scr[h_old, 0:16, c : c + rows], kh_read[c : c + rows], preferred_element_type=F32)
            acc += jnp.dot(v_scr[h_old, 16:32, c : c + rows], kl_read[c : c + rows], preferred_element_type=F32)
        target_features(i + 1, b_next)
        done = (acc[0:8] + acc[8:16]) * jnp.where((i >= 2) & (i < count + 2), GAIN, 0.0)
        at = pl.ds(pl.multiple_of((item_g[old] + (lo - base)) * leaf_size, leaf_size), leaf_size)
        out_ref[:, at] += done

    target_features(0, b0)

    def two_turns(i, _):
        turn(2 * i, b0, b1, u0, u1, kh0, kl0, kh1, kl1)
        turn(2 * i + 1, b1, b0, u1, u0, kh1, kl1, kh0, kl0)
        return 0

    lax.fori_loop(0, (count + 3) >> 1, two_turns, 0)


def near_scratch(count, slots, leaf_size):
    square = (leaf_size, leaf_size)
    leaves = count + 2 * HALO
    return [
        pltpu.VMEM((8, leaf_size), F32),
        pltpu.VMEM((leaves, 8, leaf_size), F32),
        pltpu.VMEM((leaves, leaf_size, DEPTH), BF16),
        pltpu.VMEM((leaves, 32, leaf_size), BF16),
        pltpu.VMEM((DEPTH, leaf_size), BF16),
        pltpu.VMEM((DEPTH, leaf_size), BF16),
        pltpu.VMEM(square, F32),
        pltpu.VMEM(square, F32),
        pltpu.VMEM(square, BF16),
        pltpu.VMEM(square, BF16),
        pltpu.VMEM(square, BF16),
        pltpu.VMEM(square, BF16),
        pltpu.SMEM((count * (slots + 1) + 8,), jnp.int32),
        pltpu.SMEM((count * (slots + 1) + 8,), jnp.int32),
    ]


NEAR_INPUTS = 8


def near_kernel(*refs, lo, hi, leaf_size):
    near_core(refs[:NEAR_INPUTS], refs[NEAR_INPUTS], refs[NEAR_INPUTS + 1 :], lo=lo, hi=hi, base=lo, leaf_size=leaf_size)


def near_cost(count, leaves, leaf_size):
    return pl.CostEstimate(
        flops=count * 3 * leaf_size * leaf_size * 512,
        bytes_accessed=8 * 11 * leaves * leaf_size,
        transcendentals=count * 6 * leaf_size * leaf_size,
    )


def near_specs():
    return [pl.BlockSpec(memory_space=pltpu.SMEM)] * 2 + [pl.BlockSpec(memory_space=pltpu.VMEM)] * 6


def near_field(inputs, lo, hi):
    leaves, slots = inputs[1].shape
    columns, points = inputs[3].shape
    leaf_size = points // leaves
    return pl.pallas_call(
        functools.partial(near_kernel, lo=lo, hi=hi, leaf_size=leaf_size),
        in_specs=near_specs(),
        out_specs=pl.BlockSpec(memory_space=pltpu.VMEM),
        out_shape=jax.ShapeDtypeStruct((columns, (hi - lo) * leaf_size), F32),
        scratch_shapes=near_scratch(hi - lo, slots, leaf_size),
        compiler_params=pltpu.CompilerParams(vmem_limit_bytes=NEAR_LIMIT),
        cost_estimate=near_cost(hi - lo, leaves, leaf_size),
    )(*inputs)


def last_kernel(*refs, lo, leaf_size):
    inputs = refs[:NEAR_INPUTS]
    done_ref, place_ref, target_ref, source_ref, *hbm, out_ref = refs[NEAR_INPUTS : NEAR_INPUTS + 11]
    coef, coupling, transfer, basis, down, across, local_scr, sems, *scratch = refs[NEAR_INPUTS + 11 :]
    held = (coef, coupling, transfer, basis, down, across)
    peers, slots = target_ref.shape
    leaves = basis.shape[0]
    parts = sems.shape[1]

    def copies():
        for i, (source, target) in enumerate(zip(hbm, held, strict=True)):
            number = math.gcd(parts, source.shape[0])
            size = source.shape[0] // number
            for j in range(number):
                at = pl.ds(j * size, size)
                yield pltpu.make_async_copy(source.at[at], target.at[at], sems.at[i, j])

    for copy in copies():
        copy.start()

    out_ref[:, 0 : lo * leaf_size] = done_ref[...]
    local_scr[...] = jnp.zeros_like(local_scr)
    near_core(inputs, out_ref, scratch, lo=lo, hi=leaves, base=0, leaf_size=leaf_size)

    for copy in copies():
        copy.wait()

    here = place_ref[0]
    sums = [coef[0, leaves + level] for level in range(3)]
    for p in range(1, peers):
        sums = [total + coef[p, leaves + level] for level, total in enumerate(sums)]
    region = dot_plain(sums[2], across[12 + (here >> 2)])
    region = dot_plain(sums[1], across[8 + (here >> 1)]) + dot_turned(region, down[8 + (here >> 1)])
    region = dot_plain(sums[0], across[here]) + dot_turned(region, down[here])

    def far(p, _):
        products = [dot_plain(coef[p, source_ref[p, k]], coupling[p, k]) for k in range(slots)]
        for k in range(slots):
            local_scr[target_ref[p, k]] += products[k]
        return 0

    lax.fori_loop(0, peers, far, 0)

    group = 4

    def back(i, _):
        locals_ = [local_scr[i * group + j] + dot_turned(region, transfer[i * group + j]) for j in range(group)]
        for j in range(group):
            at = pl.ds(pl.multiple_of((i * group + j) * leaf_size, leaf_size), leaf_size)
            out_ref[:, at] += dot_turned(locals_[j], basis[i * group + j])
        return 0

    lax.fori_loop(0, leaves // group, back, 0)


def last_field(inputs, done, place, targets, sources, coefs, far_coupling, leaf_transfer, leaf_basis, upper_transfer, upper_coupling):
    leaves, leaf_size, rank = leaf_basis.shape
    columns, points = inputs[3].shape
    slots = inputs[1].shape[1]
    lo = done.shape[1] // leaf_size
    smem, vmem = pl.BlockSpec(memory_space=pltpu.SMEM), pl.BlockSpec(memory_space=pltpu.VMEM)
    hbm = pl.BlockSpec(memory_space=pl.ANY)
    streamed = (coefs, far_coupling, leaf_transfer, leaf_basis, upper_transfer, upper_coupling)
    return pl.pallas_call(
        functools.partial(last_kernel, lo=lo, leaf_size=leaf_size),
        in_specs=near_specs() + [vmem, smem, smem, smem] + [hbm] * len(streamed),
        out_specs=vmem,
        out_shape=jax.ShapeDtypeStruct((columns, points), F32),
        scratch_shapes=[pltpu.VMEM(x.shape, F32) for x in streamed]
        + [pltpu.VMEM((leaves + 1, columns, rank), F32), pltpu.SemaphoreType.DMA((len(streamed), 8))]
        + near_scratch(leaves - lo, slots, leaf_size),
        compiler_params=pltpu.CompilerParams(vmem_limit_bytes=WIDE_LIMIT),
        cost_estimate=near_cost(leaves - lo, leaves, leaf_size),
    )(*inputs, done, place, targets, sources, *streamed)


def neighbours(points, vectors, width):
    axes = ("leaf", "top")
    count = lax.axis_size("leaf") * lax.axis_size("top")
    joined = [jnp.concatenate([points[:, s], vectors[:, s]], axis=0) for s in (slice(-width, None), slice(0, width))]
    before = lax.ppermute(joined[0], axes, [(i, i + 1) for i in range(count - 1)])
    after = lax.ppermute(joined[1], axes, [(i + 1, i) for i in range(count - 1)])
    return (before[:3], before[3:]), (after[:3], after[3:])


def shards(
    points,
    vectors,
    near_offset,
    leaf_basis,
    leaf_transfer,
    far_target,
    far_source,
    far_coupling,
    upper_transfer,
    upper_coupling,
):
    leaves, leaf_size, _ = leaf_basis.shape
    peers = lax.axis_size("top")
    region, peer = lax.axis_index("leaf"), lax.axis_index("top")
    place = region.astype(jnp.int32).reshape(1)
    first = ((region * peers + peer) * leaves).astype(jnp.int32).reshape(1)

    before, after = neighbours(points, vectors, HALO * leaf_size)
    coefs, parts = coefficients(place, vectors, leaf_basis, leaf_transfer, upper_transfer)
    for level, part in enumerate(siblings(parts)):
        coefs = lax.dynamic_update_slice_in_dim(coefs, part, leaves + level, 0)
    gathered = lax.all_gather(coefs, "top", axis=0)
    inputs = (first, near_offset, points, vectors, *before, *after)
    early = near_field(inputs, 0, EARLY_LEAVES)
    return last_field(
        inputs,
        early,
        place,
        far_target[0],
        far_source[0],
        gathered,
        far_coupling[0],
        leaf_transfer,
        leaf_basis,
        upper_transfer,
        upper_coupling,
    )


def solution(mesh):
    split = ("leaf", "top")
    in_specs = (
        P(None, split),
        P(None, split),
        P(split, None),
        P(split, None, None),
        P(split, None, None),
        P(split, None, None),
        P(split, None, None),
        P(split, None, None, None, None),
        P(),
        P(),
    )
    return jax.shard_map(shards, mesh=mesh, in_specs=in_specs, out_specs=P(None, split), check_vma=False)
```

```python
import functools
import math

import jax
import jax.numpy as jnp
from jax import lax
from jax.experimental import pallas as pl
from jax.experimental.pallas import tpu as pltpu
from jax.sharding import PartitionSpec as P

F32, BF16 = jnp.float32, jnp.bfloat16
NUGGET = 0.1
SCALES = (0.3, 0.15, 0.15)
LOG2E = math.log2(math.e)
FACTOR = tuple(math.sqrt(3.0) * LOG2E / scale for scale in SCALES)
GAIN = -0.25 * math.log(2.0) * math.e
TINY = 1e-20
DEPTH = 64
HALO = 2
CHUNK = 64
UNROLL = 4
NEAR_LIMIT = 20 << 20
WIDE_LIMIT = 56 << 20
EARLY_LEAVES = 30


def halves(x):
    high = x.astype(BF16)
    return high, (x - high.astype(F32)).astype(BF16)


def thirds(x):
    high = x.astype(BF16).astype(F32)
    rest = x - high
    middle = rest.astype(BF16).astype(F32)
    return high, middle, rest - middle


def dot_plain(x, matrix):
    n = matrix.shape[1]
    left = jnp.concatenate(halves(x), axis=0)
    out = jnp.dot(left, jnp.concatenate(halves(matrix), axis=1), preferred_element_type=F32)
    return out[0:8, 0:n] + out[8:16, 0:n] + out[0:8, n : 2 * n]


def dot_turned(x, matrix):
    high, low = halves(x)
    upper = jnp.concatenate([high, high], axis=1)
    lower = jnp.concatenate([low, jnp.zeros_like(low)], axis=1)
    out = lax.dot_general(
        jnp.concatenate([upper, lower], axis=0),
        jnp.concatenate(halves(matrix), axis=1),
        (((1,), (1,)), ((), ())),
        preferred_element_type=F32,
    )
    return out[0:8] + out[8:16]


def coef_kernel(place_ref, vec_hbm, basis_hbm, transfer_hbm, up0_ref, up1_ref, coef_ref, part_ref, vec, basis, transfer, sems, *, group):
    del place_ref
    leaves, leaf_size, _ = basis.shape
    groups = leaves // group

    def copies(i):
        at = pl.ds(i * group, group)
        points = pl.ds(pl.multiple_of(i * (group * leaf_size), group * leaf_size), group * leaf_size)
        return (
            pltpu.make_async_copy(vec_hbm.at[:, points], vec.at[:, points], sems.at[0, i]),
            pltpu.make_async_copy(basis_hbm.at[at], basis.at[at], sems.at[1, i]),
            pltpu.make_async_copy(transfer_hbm.at[at], transfer.at[at], sems.at[2, i]),
        )

    for i in range(groups):
        for copy in copies(i):
            copy.start()

    def turn(i, total):
        for copy in copies(i):
            copy.wait()
        coefs = []
        for j in range(group):
            at = pl.ds(pl.multiple_of((i * group + j) * leaf_size, leaf_size), leaf_size)
            coefs.append(dot_plain(vec[:, at], basis[i * group + j]))
        for j in range(group):
            coef_ref[i * group + j] = coefs[j]
            total += dot_plain(coefs[j], transfer[i * group + j])
        return total

    part = lax.fori_loop(0, groups, turn, jnp.zeros(part_ref.shape[1:], F32))
    part_ref[0] = part
    part = dot_plain(part, up0_ref[0])
    part_ref[1] = part
    part_ref[2] = dot_plain(part, up1_ref[0])


def coefficients(place, vectors, leaf_basis, leaf_transfer, upper_transfer):
    leaves, leaf_size, rank = leaf_basis.shape
    columns = vectors.shape[0]
    group = 4
    node = (1, rank, rank)
    hbm = pl.BlockSpec(memory_space=pl.ANY)
    return pl.pallas_call(
        functools.partial(coef_kernel, group=group),
        grid_spec=pltpu.PrefetchScalarGridSpec(
            num_scalar_prefetch=1,
            grid=(1,),
            in_specs=[
                hbm,
                hbm,
                hbm,
                pl.BlockSpec(node, lambda i, p: (p[0], 0, 0)),
                pl.BlockSpec(node, lambda i, p: (8 + (p[0] >> 1), 0, 0)),
            ],
            out_specs=[
                pl.BlockSpec((leaves + 3, columns, rank), lambda i, p: (0, 0, 0)),
                pl.BlockSpec((3, columns, rank), lambda i, p: (0, 0, 0)),
            ],
            scratch_shapes=[
                pltpu.VMEM(vectors.shape, F32),
                pltpu.VMEM(leaf_basis.shape, F32),
                pltpu.VMEM(leaf_transfer.shape, F32),
                pltpu.SemaphoreType.DMA((3, leaves // group)),
            ],
        ),
        out_shape=[
            jax.ShapeDtypeStruct((leaves + 3, columns, rank), F32),
            jax.ShapeDtypeStruct((3, columns, rank), F32),
        ],
        compiler_params=pltpu.CompilerParams(vmem_limit_bytes=WIDE_LIMIT),
        cost_estimate=pl.CostEstimate(
            flops=leaves * 16 * rank * (leaf_size + rank) * 4,
            bytes_accessed=4 * leaves * rank * (leaf_size + rank),
            transcendentals=0,
        ),
    )(place, vectors, leaf_basis, leaf_transfer, upper_transfer, upper_transfer)


def features(x, target):
    row = lax.broadcasted_iota(jnp.int32, x.shape, 0)
    norm = jnp.sum(x * x, axis=0, keepdims=True)
    high, middle, low = thirds(jnp.where(row < 3, x, norm))
    norm_row, one_row, factor = (4, 3, -2.0) if target else (3, 4, 1.0)

    def group(coordinates, norms):
        out = jnp.where(row < 3, coordinates * factor, 0.0)
        if norms is not None:
            out = jnp.where(row == norm_row, norms, jnp.where(row == one_row, 1.0, out))
        return out

    if target:
        groups = [group(high, high), group(middle, middle), group(high, low)]
        groups += [group(low, None), group(middle, None), group(high, None)]
    else:
        groups = [group(high, high), group(middle, middle), group(low, low)]
        groups += [group(high, None), group(high, None), group(middle, None)]
    groups += [jnp.zeros_like(x)] * (DEPTH // 8 - 6)
    return jnp.concatenate(groups, axis=0)


def matern(dist_sq):
    nt = -LOG2E - dist_sq * lax.rsqrt(dist_sq)
    return nt * jnp.exp2(nt)


def near_core(inputs, out_ref, scratch, *, lo, hi, base, leaf_size):
    first_ref, offset_ref, points_ref, vectors_ref, before_p, before_v, after_p, after_v = inputs
    wide_scr, x_scr, a_scr, v_scr, b0, b1, u_scr, kh_scr, kl_scr, item_g, item_h = scratch
    leaves = offset_ref.shape[0]
    first = first_ref[0]
    row8 = lax.broadcasted_iota(jnp.int32, (8, leaf_size), 0)

    wide_scr[...] = jnp.zeros_like(wide_scr)

    def prepare(p_ref, v_ref, start, stop, origin):
        def turn(h, _):
            at = pl.ds(pl.multiple_of((h - origin) * leaf_size, leaf_size), leaf_size)
            to = h + HALO - lo
            centre = (first + h).astype(F32) * 0.5 + 0.5
            wide_scr[0:3] = p_ref[:, at]
            shift = jnp.where(row8 == 0, centre, 0.5)
            scale = jnp.where(row8 == 0, FACTOR[0], FACTOR[1])
            x = jnp.where(row8 < 3, (wide_scr[...] - shift) * scale, 0.0)
            x_scr[to] = x
            a_scr[to] = features(x, False).T.astype(BF16)
            v_high, v_low = halves(v_ref[:, at])
            v_scr[to, 0:16] = jnp.concatenate([v_high, v_low], axis=0)
            v_scr[to, 16:32] = jnp.concatenate([v_high, jnp.zeros_like(v_high)], axis=0)
            return 0

        lax.fori_loop(start, stop, turn, 0)

    if lo < HALO:
        prepare(before_p, before_v, -HALO, 0, -HALO)
    prepare(points_ref, vectors_ref, max(lo - HALO, 0), min(hi + HALO, leaves), 0)
    if hi > leaves - HALO:
        prepare(after_p, after_v, leaves, leaves + HALO, leaves)

    def listing(g, n):
        at = pl.ds(pl.multiple_of(g * leaf_size, leaf_size), leaf_size)
        to = pl.ds(pl.multiple_of((g - base) * leaf_size, leaf_size), leaf_size)
        out_ref[:, to] = NUGGET * vectors_ref[:, at]
        item_g[n] = g - lo
        item_h[n] = g - lo + HALO
        n = n + 1
        for j in range(offset_ref.shape[1]):
            offset = offset_ref[g, j]
            item_g[n] = g - lo
            item_h[n] = g - lo + HALO + offset
            n = n + jnp.where(offset != 0, 1, 0)
        return n

    count = lax.fori_loop(lo, hi, listing, 0)

    def target_features(i, b_scr):
        i = jnp.minimum(i, count - 1)
        g, h = item_g[i], item_h[i]
        apart = (g + HALO - h).astype(F32) * (0.5 * FACTOR[0])
        x = x_scr[g + HALO]
        b_scr[...] = features(jnp.where(row8 == 0, x + apart, x), True).astype(BF16)

    def distances(i, b_scr, c, size):
        h = item_h[jnp.minimum(i, count - 1)]
        dist_sq = jnp.dot(a_scr[h, c : c + size], b_scr[...], preferred_element_type=F32)
        u_scr[c : c + size] = jnp.maximum(dist_sq, TINY)

    def turn(i, b_next, b_later):
        now = jnp.minimum(i, count - 1)
        h = item_h[now]
        acc = jnp.zeros((16, leaf_size), F32)
        size = CHUNK
        for c in range(0, leaf_size, size):
            for r in range(c, c + size, 32):
                high, low = halves(matern(u_scr[r : r + 32]))
                kh_scr[r : r + 32] = high
                kl_scr[r : r + 32] = low
            distances(i + 1, b_next, c, size)
            acc += jnp.dot(v_scr[h, 0:16, c : c + size], kh_scr[c : c + size], preferred_element_type=F32)
            acc += jnp.dot(v_scr[h, 16:32, c : c + size], kl_scr[c : c + size], preferred_element_type=F32)
        target_features(i + 2, b_later)
        done = jnp.where(i < count, (acc[0:8] + acc[8:16]) * GAIN, 0.0)
        at = pl.ds(pl.multiple_of((item_g[now] + (lo - base)) * leaf_size, leaf_size), leaf_size)
        out_ref[:, at] += done

    target_features(0, b0)
    target_features(1, b1)
    distances(0, b0, 0, leaf_size)

    def turns(i, _):
        for j in range(0, UNROLL, 2):
            turn(UNROLL * i + j, b1, b0)
            turn(UNROLL * i + j + 1, b0, b1)
        return 0

    lax.fori_loop(0, (count + (UNROLL - 1)) >> UNROLL.bit_length() - 1, turns, 0)


def near_scratch(count, slots, leaf_size):
    square = (leaf_size, leaf_size)
    leaves = count + 2 * HALO
    return [
        pltpu.VMEM((8, leaf_size), F32),
        pltpu.VMEM((leaves, 8, leaf_size), F32),
        pltpu.VMEM((leaves, leaf_size, DEPTH), BF16),
        pltpu.VMEM((leaves, 32, leaf_size), BF16),
        pltpu.VMEM((DEPTH, leaf_size), BF16),
        pltpu.VMEM((DEPTH, leaf_size), BF16),
        pltpu.VMEM(square, F32),
        pltpu.VMEM(square, BF16),
        pltpu.VMEM(square, BF16),
        pltpu.SMEM((count * (slots + 1) + 8,), jnp.int32),
        pltpu.SMEM((count * (slots + 1) + 8,), jnp.int32),
    ]


NEAR_INPUTS = 8


def near_kernel(*refs, lo, hi, leaf_size):
    near_core(refs[:NEAR_INPUTS], refs[NEAR_INPUTS], refs[NEAR_INPUTS + 1 :], lo=lo, hi=hi, base=lo, leaf_size=leaf_size)


def near_cost(count, leaves, leaf_size):
    return pl.CostEstimate(
        flops=count * 3 * leaf_size * leaf_size * 512,
        bytes_accessed=8 * 11 * leaves * leaf_size,
        transcendentals=count * 6 * leaf_size * leaf_size,
    )


def near_specs():
    return [pl.BlockSpec(memory_space=pltpu.SMEM)] * 2 + [pl.BlockSpec(memory_space=pltpu.VMEM)] * 6


def near_field(inputs, lo, hi):
    leaves, slots = inputs[1].shape
    columns, points = inputs[3].shape
    leaf_size = points // leaves
    return pl.pallas_call(
        functools.partial(near_kernel, lo=lo, hi=hi, leaf_size=leaf_size),
        in_specs=near_specs(),
        out_specs=pl.BlockSpec(memory_space=pltpu.VMEM),
        out_shape=jax.ShapeDtypeStruct((columns, (hi - lo) * leaf_size), F32),
        scratch_shapes=near_scratch(hi - lo, slots, leaf_size),
        compiler_params=pltpu.CompilerParams(vmem_limit_bytes=NEAR_LIMIT),
        cost_estimate=near_cost(hi - lo, leaves, leaf_size),
    )(*inputs)


def last_kernel(*refs, lo, leaf_size):
    inputs = refs[:NEAR_INPUTS]
    done_ref, place_ref, target_ref, source_ref, *hbm, out_ref = refs[NEAR_INPUTS : NEAR_INPUTS + 11]
    coef, coupling, transfer, basis, down, across, local_scr, sems, *scratch = refs[NEAR_INPUTS + 11 :]
    held = (coef, coupling, transfer, basis, down, across)
    peers, slots = target_ref.shape
    leaves = basis.shape[0]
    parts = sems.shape[1]

    def copies():
        for i, (source, target) in enumerate(zip(hbm, held, strict=True)):
            number = math.gcd(parts, source.shape[0])
            size = source.shape[0] // number
            for j in range(number):
                at = pl.ds(j * size, size)
                yield pltpu.make_async_copy(source.at[at], target.at[at], sems.at[i, j])

    for copy in copies():
        copy.start()

    out_ref[:, 0 : lo * leaf_size] = done_ref[...]
    local_scr[...] = jnp.zeros_like(local_scr)
    near_core(inputs, out_ref, scratch, lo=lo, hi=leaves, base=0, leaf_size=leaf_size)

    for copy in copies():
        copy.wait()

    here = place_ref[0]
    sums = [coef[0, leaves + level] for level in range(3)]
    for p in range(1, peers):
        sums = [total + coef[p, leaves + level] for level, total in enumerate(sums)]
    region = dot_plain(sums[2], across[12 + (here >> 2)])
    region = dot_plain(sums[1], across[8 + (here >> 1)]) + dot_turned(region, down[8 + (here >> 1)])
    region = dot_plain(sums[0], across[here]) + dot_turned(region, down[here])

    def far(p, _):
        products = [dot_plain(coef[p, source_ref[p, k]], coupling[p, k]) for k in range(slots)]
        for k in range(slots):
            local_scr[target_ref[p, k]] += products[k]
        return 0

    lax.fori_loop(0, peers, far, 0)

    group = 4

    def back(i, _):
        locals_ = [local_scr[i * group + j] + dot_turned(region, transfer[i * group + j]) for j in range(group)]
        for j in range(group):
            at = pl.ds(pl.multiple_of((i * group + j) * leaf_size, leaf_size), leaf_size)
            out_ref[:, at] += dot_turned(locals_[j], basis[i * group + j])
        return 0

    lax.fori_loop(0, leaves // group, back, 0)


def last_field(inputs, done, place, targets, sources, coefs, far_coupling, leaf_transfer, leaf_basis, upper_transfer, upper_coupling):
    leaves, leaf_size, rank = leaf_basis.shape
    columns, points = inputs[3].shape
    slots = inputs[1].shape[1]
    lo = done.shape[1] // leaf_size
    smem, vmem = pl.BlockSpec(memory_space=pltpu.SMEM), pl.BlockSpec(memory_space=pltpu.VMEM)
    hbm = pl.BlockSpec(memory_space=pl.ANY)
    streamed = (coefs, far_coupling, leaf_transfer, leaf_basis, upper_transfer, upper_coupling)
    return pl.pallas_call(
        functools.partial(last_kernel, lo=lo, leaf_size=leaf_size),
        in_specs=near_specs() + [vmem, smem, smem, smem] + [hbm] * len(streamed),
        out_specs=vmem,
        out_shape=jax.ShapeDtypeStruct((columns, points), F32),
        scratch_shapes=[pltpu.VMEM(x.shape, F32) for x in streamed]
        + [pltpu.VMEM((leaves + 1, columns, rank), F32), pltpu.SemaphoreType.DMA((len(streamed), 8))]
        + near_scratch(leaves - lo, slots, leaf_size),
        compiler_params=pltpu.CompilerParams(vmem_limit_bytes=WIDE_LIMIT),
        cost_estimate=near_cost(leaves - lo, leaves, leaf_size),
    )(*inputs, done, place, targets, sources, *streamed)


def exchange(points, vectors, parts, width):
    axes = ("leaf", "top")
    regions = lax.axis_size("leaf")
    count = regions * lax.axis_size("top")
    head, tail = (jnp.concatenate([points[:, s], vectors[:, s]], axis=0) for s in (slice(0, width), slice(-width, None)))

    def from_partner(x, distance):
        return lax.ppermute(x, "leaf", [(i, i ^ distance) for i in range(regions)])

    parts, head, tail = lax.optimization_barrier((parts, head, tail))
    before = lax.ppermute(tail, axes, [(i, i + 1) for i in range(count - 1)])
    other = from_partner(parts, 1)
    before, other, head = lax.optimization_barrier((before, other, head))
    level0, parts = other[0:1], parts[1:] + other[1:]
    after = lax.ppermute(head, axes, [(i + 1, i) for i in range(count - 1)])
    other = from_partner(parts, 2)
    after, other = lax.optimization_barrier((after, other))
    level1, parts = other[0:1], parts[1:] + other[1:]
    level2 = from_partner(parts, 4)
    return (before[:3], before[3:]), (after[:3], after[3:]), (level0, level1, level2)


def shards(
    points,
    vectors,
    near_offset,
    leaf_basis,
    leaf_transfer,
    far_target,
    far_source,
    far_coupling,
    upper_transfer,
    upper_coupling,
):
    leaves, leaf_size, _ = leaf_basis.shape
    peers = lax.axis_size("top")
    region, peer = lax.axis_index("leaf"), lax.axis_index("top")
    place = region.astype(jnp.int32).reshape(1)
    first = ((region * peers + peer) * leaves).astype(jnp.int32).reshape(1)

    coefs, parts = coefficients(place, vectors, leaf_basis, leaf_transfer, upper_transfer)
    before, after, levels = exchange(points, vectors, parts, HALO * leaf_size)
    coefs = lax.dynamic_update_slice_in_dim(coefs, jnp.concatenate(levels), leaves, 0)
    gathered = lax.all_gather(coefs, "top", axis=0)
    inputs = (first, near_offset, points, vectors, *before, *after)
    early = near_field(inputs, 0, EARLY_LEAVES)
    return last_field(
        inputs,
        early,
        place,
        far_target[0],
        far_source[0],
        gathered,
        far_coupling[0],
        leaf_transfer,
        leaf_basis,
        upper_transfer,
        upper_coupling,
    )


def solution(mesh):
    split = ("leaf", "top")
    in_specs = (
        P(None, split),
        P(None, split),
        P(split, None),
        P(split, None, None),
        P(split, None, None),
        P(split, None, None),
        P(split, None, None),
        P(split, None, None, None, None),
        P(),
        P(),
    )
    return jax.shard_map(shards, mesh=mesh, in_specs=in_specs, out_specs=P(None, split), check_vma=False)
```

```python
import functools
import math

import jax
import jax.numpy as jnp
from jax import lax
from jax.experimental import pallas as pl
from jax.experimental.pallas import tpu as pltpu
from jax.sharding import PartitionSpec as P

F32, BF16 = jnp.float32, jnp.bfloat16
NUGGET = 0.1
SCALES = (0.3, 0.15, 0.15)
LOG2E = math.log2(math.e)
FACTOR = tuple(math.sqrt(3.0) * LOG2E / scale for scale in SCALES)
GAIN = -0.25 * math.log(2.0) * math.e
TINY = 1e-20
DEPTH = 64
HALO = 2
CHUNK = 64
UNROLL = 4
NEAR_LIMIT = 20 << 20
WIDE_LIMIT = 56 << 20
LAST_LIMIT = 56 << 20
EARLY_LEAVES = 32


def halves(x):
    high = x.astype(BF16)
    return high, (x - high.astype(F32)).astype(BF16)


def thirds(x):
    high = x.astype(BF16).astype(F32)
    rest = x - high
    middle = rest.astype(BF16).astype(F32)
    return high, middle, rest - middle


def dot_plain(x, matrix):
    n = matrix.shape[1]
    left = jnp.concatenate(halves(x), axis=0)
    out = jnp.dot(left, jnp.concatenate(halves(matrix), axis=1), preferred_element_type=F32)
    return out[0:8, 0:n] + out[8:16, 0:n] + out[0:8, n : 2 * n]


def dot_turned(x, matrix):
    high, low = halves(x)
    upper = jnp.concatenate([high, high], axis=1)
    lower = jnp.concatenate([low, jnp.zeros_like(low)], axis=1)
    out = lax.dot_general(
        jnp.concatenate([upper, lower], axis=0),
        jnp.concatenate(halves(matrix), axis=1),
        (((1,), (1,)), ((), ())),
        preferred_element_type=F32,
    )
    return out[0:8] + out[8:16]


def coef_kernel(place_ref, vec_hbm, basis_hbm, transfer_hbm, up0_ref, up1_ref, coef_ref, vec, basis, transfer, sems, *, group):
    del place_ref
    leaves, leaf_size, _ = basis.shape
    groups = leaves // group

    def copies(i):
        at = pl.ds(i * group, group)
        points = pl.ds(pl.multiple_of(i * (group * leaf_size), group * leaf_size), group * leaf_size)
        return (
            pltpu.make_async_copy(vec_hbm.at[:, points], vec.at[:, points], sems.at[0, i]),
            pltpu.make_async_copy(basis_hbm.at[at], basis.at[at], sems.at[1, i]),
            pltpu.make_async_copy(transfer_hbm.at[at], transfer.at[at], sems.at[2, i]),
        )

    for i in range(groups):
        for copy in copies(i):
            copy.start()

    def turn(i, total):
        for copy in copies(i):
            copy.wait()
        coefs = []
        for j in range(group):
            at = pl.ds(pl.multiple_of((i * group + j) * leaf_size, leaf_size), leaf_size)
            coefs.append(dot_plain(vec[:, at], basis[i * group + j]))
        for j in range(group):
            coef_ref[i * group + j] = coefs[j]
            total += dot_plain(coefs[j], transfer[i * group + j])
        return total

    part = lax.fori_loop(0, groups, turn, jnp.zeros(coef_ref.shape[1:], F32))
    coef_ref[leaves] = part
    part = dot_plain(part, up0_ref[0])
    coef_ref[leaves + 1] = part
    coef_ref[leaves + 2] = dot_plain(part, up1_ref[0])


def coefficients(place, vectors, leaf_basis, leaf_transfer, upper_transfer):
    leaves, leaf_size, rank = leaf_basis.shape
    columns = vectors.shape[0]
    group = 4
    node = (1, rank, rank)
    hbm = pl.BlockSpec(memory_space=pl.ANY)
    return pl.pallas_call(
        functools.partial(coef_kernel, group=group),
        grid_spec=pltpu.PrefetchScalarGridSpec(
            num_scalar_prefetch=1,
            grid=(1,),
            in_specs=[
                hbm,
                hbm,
                hbm,
                pl.BlockSpec(node, lambda i, p: (p[0], 0, 0)),
                pl.BlockSpec(node, lambda i, p: (8 + (p[0] >> 1), 0, 0)),
            ],
            out_specs=pl.BlockSpec((leaves + 3, columns, rank), lambda i, p: (0, 0, 0)),
            scratch_shapes=[
                pltpu.VMEM(vectors.shape, F32),
                pltpu.VMEM(leaf_basis.shape, F32),
                pltpu.VMEM(leaf_transfer.shape, F32),
                pltpu.SemaphoreType.DMA((3, leaves // group)),
            ],
        ),
        out_shape=jax.ShapeDtypeStruct((leaves + 3, columns, rank), F32),
        compiler_params=pltpu.CompilerParams(vmem_limit_bytes=WIDE_LIMIT),
        cost_estimate=pl.CostEstimate(
            flops=leaves * 16 * rank * (leaf_size + rank) * 4,
            bytes_accessed=4 * leaves * rank * (leaf_size + rank),
            transcendentals=0,
        ),
    )(place, vectors, leaf_basis, leaf_transfer, upper_transfer, upper_transfer)


def features(x, target):
    row = lax.broadcasted_iota(jnp.int32, x.shape, 0)
    norm = jnp.sum(x * x, axis=0, keepdims=True)
    high, middle, low = thirds(jnp.where(row < 3, x, norm))
    norm_row, one_row, factor = (4, 3, -2.0) if target else (3, 4, 1.0)

    def group(coordinates, norms):
        out = jnp.where(row < 3, coordinates * factor, 0.0)
        if norms is not None:
            out = jnp.where(row == norm_row, norms, jnp.where(row == one_row, 1.0, out))
        return out

    if target:
        groups = [group(high, high), group(middle, middle), group(high, low)]
        groups += [group(low, None), group(middle, None), group(high, None)]
    else:
        groups = [group(high, high), group(middle, middle), group(low, low)]
        groups += [group(high, None), group(high, None), group(middle, None)]
    groups += [jnp.zeros_like(x)] * (DEPTH // 8 - 6)
    return jnp.concatenate(groups, axis=0)


def matern(dist_sq):
    nt = -LOG2E - dist_sq * lax.rsqrt(dist_sq)
    return nt * jnp.exp2(nt)


def near_core(inputs, out_ref, scratch, *, lo, hi, base, leaf_size):
    first_ref, offset_ref, points_ref, vectors_ref, before_p, before_v, after_p, after_v = inputs
    wide_scr, x_scr, a_scr, v_scr, b0, b1, u_scr, kh_scr, kl_scr, item_g, item_h = scratch
    leaves = offset_ref.shape[0]
    first = first_ref[0]
    row8 = lax.broadcasted_iota(jnp.int32, (8, leaf_size), 0)

    wide_scr[...] = jnp.zeros_like(wide_scr)

    def prepare(p_ref, v_ref, start, stop, origin):
        def turn(h, _):
            at = pl.ds(pl.multiple_of((h - origin) * leaf_size, leaf_size), leaf_size)
            to = h + HALO - lo
            centre = (first + h).astype(F32) * 0.5 + 0.5
            wide_scr[0:3] = p_ref[:, at]
            shift = jnp.where(row8 == 0, centre, 0.5)
            scale = jnp.where(row8 == 0, FACTOR[0], FACTOR[1])
            x = jnp.where(row8 < 3, (wide_scr[...] - shift) * scale, 0.0)
            x_scr[to] = x
            a_scr[to] = features(x, False).T.astype(BF16)
            v_high, v_low = halves(v_ref[:, at])
            v_scr[to, 0:16] = jnp.concatenate([v_high, v_low], axis=0)
            v_scr[to, 16:32] = jnp.concatenate([v_high, jnp.zeros_like(v_high)], axis=0)
            return 0

        lax.fori_loop(start, stop, turn, 0)

    if lo < HALO:
        prepare(before_p, before_v, -HALO, 0, -HALO)
    prepare(points_ref, vectors_ref, max(lo - HALO, 0), min(hi + HALO, leaves), 0)
    if hi > leaves - HALO:
        prepare(after_p, after_v, leaves, leaves + HALO, leaves)

    def listing(g, n):
        at = pl.ds(pl.multiple_of(g * leaf_size, leaf_size), leaf_size)
        to = pl.ds(pl.multiple_of((g - base) * leaf_size, leaf_size), leaf_size)
        out_ref[:, to] = NUGGET * vectors_ref[:, at]
        item_g[n] = g - lo
        item_h[n] = g - lo + HALO
        n = n + 1
        for j in range(offset_ref.shape[1]):
            offset = offset_ref[g, j]
            item_g[n] = g - lo
            item_h[n] = g - lo + HALO + offset
            n = n + jnp.where(offset != 0, 1, 0)
        return n

    count = lax.fori_loop(lo, hi, listing, 0)

    def target_features(i, b_scr):
        i = jnp.minimum(i, count - 1)
        g, h = item_g[i], item_h[i]
        apart = (g + HALO - h).astype(F32) * (0.5 * FACTOR[0])
        x = x_scr[g + HALO]
        b_scr[...] = features(jnp.where(row8 == 0, x + apart, x), True).astype(BF16)

    def distances(i, b_scr, c, size):
        h = item_h[jnp.minimum(i, count - 1)]
        dist_sq = jnp.dot(a_scr[h, c : c + size], b_scr[...], preferred_element_type=F32)
        u_scr[c : c + size] = jnp.maximum(dist_sq, TINY)

    def turn(i, b_next, b_later):
        now = jnp.minimum(i, count - 1)
        h = item_h[now]
        acc = jnp.zeros((16, leaf_size), F32)
        size = CHUNK
        for c in range(0, leaf_size, size):
            for r in range(c, c + size, 32):
                high, low = halves(matern(u_scr[r : r + 32]))
                kh_scr[r : r + 32] = high
                kl_scr[r : r + 32] = low
            distances(i + 1, b_next, c, size)
            acc += jnp.dot(v_scr[h, 0:16, c : c + size], kh_scr[c : c + size], preferred_element_type=F32)
            acc += jnp.dot(v_scr[h, 16:32, c : c + size], kl_scr[c : c + size], preferred_element_type=F32)
        target_features(i + 2, b_later)
        done = jnp.where(i < count, (acc[0:8] + acc[8:16]) * GAIN, 0.0)
        at = pl.ds(pl.multiple_of((item_g[now] + (lo - base)) * leaf_size, leaf_size), leaf_size)
        out_ref[:, at] += done

    target_features(0, b0)
    target_features(1, b1)
    distances(0, b0, 0, leaf_size)

    def turns(i, _):
        for j in range(0, UNROLL, 2):
            turn(UNROLL * i + j, b1, b0)
            turn(UNROLL * i + j + 1, b0, b1)
        return 0

    lax.fori_loop(0, (count + (UNROLL - 1)) >> UNROLL.bit_length() - 1, turns, 0)


def near_scratch(count, slots, leaf_size):
    square = (leaf_size, leaf_size)
    leaves = count + 2 * HALO
    return [
        pltpu.VMEM((8, leaf_size), F32),
        pltpu.VMEM((leaves, 8, leaf_size), F32),
        pltpu.VMEM((leaves, leaf_size, DEPTH), BF16),
        pltpu.VMEM((leaves, 32, leaf_size), BF16),
        pltpu.VMEM((DEPTH, leaf_size), BF16),
        pltpu.VMEM((DEPTH, leaf_size), BF16),
        pltpu.VMEM(square, F32),
        pltpu.VMEM(square, BF16),
        pltpu.VMEM(square, BF16),
        pltpu.SMEM((count * (slots + 1) + 8,), jnp.int32),
        pltpu.SMEM((count * (slots + 1) + 8,), jnp.int32),
    ]


NEAR_INPUTS = 8


def near_kernel(*refs, lo, hi, leaf_size):
    near_core(refs[:NEAR_INPUTS], refs[NEAR_INPUTS], refs[NEAR_INPUTS + 1 :], lo=lo, hi=hi, base=lo, leaf_size=leaf_size)


def near_cost(count, leaves, leaf_size):
    return pl.CostEstimate(
        flops=count * 3 * leaf_size * leaf_size * 512,
        bytes_accessed=8 * 11 * leaves * leaf_size,
        transcendentals=count * 6 * leaf_size * leaf_size,
    )


def near_specs():
    return [pl.BlockSpec(memory_space=pltpu.SMEM)] * 2 + [pl.BlockSpec(memory_space=pltpu.VMEM)] * 6


def near_field(inputs, lo, hi):
    leaves, slots = inputs[1].shape
    columns, points = inputs[3].shape
    leaf_size = points // leaves
    return pl.pallas_call(
        functools.partial(near_kernel, lo=lo, hi=hi, leaf_size=leaf_size),
        in_specs=near_specs(),
        out_specs=pl.BlockSpec(memory_space=pltpu.VMEM),
        out_shape=jax.ShapeDtypeStruct((columns, (hi - lo) * leaf_size), F32),
        scratch_shapes=near_scratch(hi - lo, slots, leaf_size),
        compiler_params=pltpu.CompilerParams(vmem_limit_bytes=NEAR_LIMIT),
        cost_estimate=near_cost(hi - lo, leaves, leaf_size),
    )(*inputs)


def last_kernel(*refs, lo, leaf_size):
    inputs = refs[:NEAR_INPUTS]
    done_ref, place_ref, slot_ref, level0, level1, level2, *hbm, out_ref = refs[NEAR_INPUTS : NEAR_INPUTS + 13]
    coef, coupling, transfer, basis, down, across, local_scr, sems, *scratch = refs[NEAR_INPUTS + 13 :]
    held = (coef, coupling, transfer, basis, down, across)
    peers, slots, _, _ = coupling.shape
    leaves = basis.shape[0]
    parts = sems.shape[1]

    def copies():
        for i, (source, target) in enumerate(zip(hbm, held, strict=True)):
            number = math.gcd(parts, source.shape[0])
            size = source.shape[0] // number
            for j in range(number):
                at = pl.ds(j * size, size)
                yield pltpu.make_async_copy(source.at[at], target.at[at], sems.at[i, j])

    for copy in copies():
        copy.start()

    out_ref[:, 0 : lo * leaf_size] = done_ref[...]
    local_scr[...] = jnp.zeros_like(local_scr)
    near_core(inputs, out_ref, scratch, lo=lo, hi=leaves, base=0, leaf_size=leaf_size)

    for copy in copies():
        copy.wait()

    here = place_ref[0]
    region = dot_plain(level2[0], across[12 + (here >> 2)])
    region = dot_plain(level1[0], across[8 + (here >> 1)]) + dot_turned(region, down[8 + (here >> 1)])
    region = dot_plain(level0[0], across[here]) + dot_turned(region, down[here])

    def far(p, _):
        products = [dot_plain(coef[p, slot_ref[peers + p, k]], coupling[p, k]) for k in range(slots)]
        for k in range(slots):
            local_scr[slot_ref[p, k]] += products[k]
        return 0

    lax.fori_loop(0, peers, far, 0)

    group = 4

    def back(i, _):
        locals_ = [local_scr[i * group + j] + dot_turned(region, transfer[i * group + j]) for j in range(group)]
        for j in range(group):
            at = pl.ds(pl.multiple_of((i * group + j) * leaf_size, leaf_size), leaf_size)
            out_ref[:, at] += dot_turned(locals_[j], basis[i * group + j])
        return 0

    lax.fori_loop(0, leaves // group, back, 0)


def last_field(inputs, done, place, slots_of, levels, coefs, far_coupling, leaf_transfer, leaf_basis, upper_transfer, upper_coupling):
    leaves, leaf_size, rank = leaf_basis.shape
    columns, points = inputs[3].shape
    slots = inputs[1].shape[1]
    lo = done.shape[1] // leaf_size
    smem, vmem = pl.BlockSpec(memory_space=pltpu.SMEM), pl.BlockSpec(memory_space=pltpu.VMEM)
    hbm = pl.BlockSpec(memory_space=pl.ANY)
    streamed = (coefs, far_coupling, leaf_transfer, leaf_basis, upper_transfer, upper_coupling)
    return pl.pallas_call(
        functools.partial(last_kernel, lo=lo, leaf_size=leaf_size),
        in_specs=near_specs() + [vmem, smem, smem, vmem, vmem, vmem] + [hbm] * len(streamed),
        out_specs=vmem,
        out_shape=jax.ShapeDtypeStruct((columns, points), F32),
        scratch_shapes=[pltpu.VMEM(x.shape, F32) for x in streamed]
        + [pltpu.VMEM((leaves + 1, columns, rank), F32), pltpu.SemaphoreType.DMA((len(streamed), 8))]
        + near_scratch(leaves - lo, slots, leaf_size),
        compiler_params=pltpu.CompilerParams(vmem_limit_bytes=LAST_LIMIT),
        cost_estimate=near_cost(leaves - lo, leaves, leaf_size),
    )(*inputs, done, place, slots_of, *levels, *streamed)


def neighbours(points, vectors, width):
    axes = ("leaf", "top")
    count = lax.axis_size("leaf") * lax.axis_size("top")
    head, tail = (jnp.concatenate([points[:, s], vectors[:, s]], axis=0) for s in (slice(0, width), slice(-width, None)))
    before = lax.ppermute(tail, axes, [(i, i + 1) for i in range(count - 1)])
    after = lax.ppermute(head, axes, [(i + 1, i) for i in range(count - 1)])
    return (before[:3], before[3:]), (after[:3], after[3:])


def siblings(sums):
    count = lax.axis_size("leaf")

    def from_partner(x, distance):
        return lax.ppermute(x, "leaf", [(i, i ^ distance) for i in range(count)])

    other = from_partner(sums, 1)
    level0, sums = other[0:1], sums[1:] + other[1:]
    other = from_partner(sums, 2)
    level1, sums = other[0:1], sums[1:] + other[1:]
    return level0, level1, from_partner(sums, 4)


def shards(
    points,
    vectors,
    near_offset,
    leaf_basis,
    leaf_transfer,
    far_target,
    far_source,
    far_coupling,
    upper_transfer,
    upper_coupling,
):
    leaves, leaf_size, _ = leaf_basis.shape
    peers = lax.axis_size("top")
    region, peer = lax.axis_index("leaf"), lax.axis_index("top")
    place = region.astype(jnp.int32).reshape(1)
    first = ((region * peers + peer) * leaves).astype(jnp.int32).reshape(1)

    coefs = coefficients(place, vectors, leaf_basis, leaf_transfer, upper_transfer)
    gathered = lax.all_gather(coefs, "top", axis=0)
    before, after = neighbours(points, vectors, HALO * leaf_size)
    inputs = (first, near_offset, points, vectors, *before, *after)
    early = near_field(inputs, 0, EARLY_LEAVES)
    gathered, early = lax.optimization_barrier((gathered, early))
    levels = siblings(jnp.sum(gathered[:, leaves:], axis=0))
    return last_field(
        inputs,
        early,
        place,
        jnp.concatenate([far_target[0], far_source[0]], axis=0),
        levels,
        gathered,
        far_coupling[0],
        leaf_transfer,
        leaf_basis,
        upper_transfer,
        upper_coupling,
    )


def solution(mesh):
    split = ("leaf", "top")
    in_specs = (
        P(None, split),
        P(None, split),
        P(split, None),
        P(split, None, None),
        P(split, None, None),
        P(split, None, None),
        P(split, None, None),
        P(split, None, None, None, None),
        P(),
        P(),
    )
    return jax.shard_map(shards, mesh=mesh, in_specs=in_specs, out_specs=P(None, split), check_vma=False)
```

```python
import functools
import math

import jax
import jax.numpy as jnp
from jax import lax
from jax.experimental import pallas as pl
from jax.experimental.pallas import tpu as pltpu
from jax.sharding import PartitionSpec as P

F32, BF16 = jnp.float32, jnp.bfloat16
NUGGET = 0.1
SCALES = (0.3, 0.15, 0.15)
LOG2E = math.log2(math.e)
FACTOR = tuple(math.sqrt(3.0) * LOG2E / scale for scale in SCALES)
GAIN = -0.25 * math.log(2.0) * math.e
TINY = 1e-20
DEPTH = 64
HALO = 2
CHUNK = 64
UNROLL = 4
NEAR_LIMIT = 20 << 20
WIDE_LIMIT = 56 << 20
LAST_LIMIT = 56 << 20
EARLY_LEAVES = 32


def halves(x):
    high = x.astype(BF16)
    return high, (x - high.astype(F32)).astype(BF16)


def thirds(x):
    high = x.astype(BF16).astype(F32)
    rest = x - high
    middle = rest.astype(BF16).astype(F32)
    return high, middle, rest - middle


def dot_plain(x, matrix):
    n = matrix.shape[1]
    left = jnp.concatenate(halves(x), axis=0)
    out = jnp.dot(left, jnp.concatenate(halves(matrix), axis=1), preferred_element_type=F32)
    return out[0:8, 0:n] + out[8:16, 0:n] + out[0:8, n : 2 * n]


def dot_turned(x, matrix):
    high, low = halves(x)
    upper = jnp.concatenate([high, high], axis=1)
    lower = jnp.concatenate([low, jnp.zeros_like(low)], axis=1)
    out = lax.dot_general(
        jnp.concatenate([upper, lower], axis=0),
        jnp.concatenate(halves(matrix), axis=1),
        (((1,), (1,)), ((), ())),
        preferred_element_type=F32,
    )
    return out[0:8] + out[8:16]


def coef_kernel(place_ref, vec_hbm, basis_hbm, transfer_hbm, up0_ref, up1_ref, coef_ref, vec, basis, transfer, sems, *, group):
    del place_ref
    leaves, leaf_size, _ = basis.shape
    groups = leaves // group

    def copies(i):
        at = pl.ds(i * group, group)
        points = pl.ds(pl.multiple_of(i * (group * leaf_size), group * leaf_size), group * leaf_size)
        return (
            pltpu.make_async_copy(vec_hbm.at[:, points], vec.at[:, points], sems.at[0, i]),
            pltpu.make_async_copy(basis_hbm.at[at], basis.at[at], sems.at[1, i]),
            pltpu.make_async_copy(transfer_hbm.at[at], transfer.at[at], sems.at[2, i]),
        )

    for i in range(groups):
        for copy in copies(i):
            copy.start()

    def turn(i, total):
        for copy in copies(i):
            copy.wait()
        coefs = []
        for j in range(group):
            at = pl.ds(pl.multiple_of((i * group + j) * leaf_size, leaf_size), leaf_size)
            coefs.append(dot_plain(vec[:, at], basis[i * group + j]))
        for j in range(group):
            coef_ref[i * group + j] = coefs[j]
            total += dot_plain(coefs[j], transfer[i * group + j])
        return total

    part = lax.fori_loop(0, groups, turn, jnp.zeros(coef_ref.shape[1:], F32))
    coef_ref[leaves] = part
    part = dot_plain(part, up0_ref[0])
    coef_ref[leaves + 1] = part
    coef_ref[leaves + 2] = dot_plain(part, up1_ref[0])


def coefficients(place, vectors, leaf_basis, leaf_transfer, upper_transfer):
    leaves, leaf_size, rank = leaf_basis.shape
    columns = vectors.shape[0]
    group = 4
    node = (1, rank, rank)
    hbm = pl.BlockSpec(memory_space=pl.ANY)
    return pl.pallas_call(
        functools.partial(coef_kernel, group=group),
        grid_spec=pltpu.PrefetchScalarGridSpec(
            num_scalar_prefetch=1,
            grid=(1,),
            in_specs=[
                hbm,
                hbm,
                hbm,
                pl.BlockSpec(node, lambda i, p: (p[0], 0, 0)),
                pl.BlockSpec(node, lambda i, p: (8 + (p[0] >> 1), 0, 0)),
            ],
            out_specs=pl.BlockSpec((leaves + 3, columns, rank), lambda i, p: (0, 0, 0)),
            scratch_shapes=[
                pltpu.VMEM(vectors.shape, F32),
                pltpu.VMEM(leaf_basis.shape, F32),
                pltpu.VMEM(leaf_transfer.shape, F32),
                pltpu.SemaphoreType.DMA((3, leaves // group)),
            ],
        ),
        out_shape=jax.ShapeDtypeStruct((leaves + 3, columns, rank), F32),
        compiler_params=pltpu.CompilerParams(vmem_limit_bytes=WIDE_LIMIT),
        cost_estimate=pl.CostEstimate(
            flops=leaves * 16 * rank * (leaf_size + rank) * 4,
            bytes_accessed=4 * leaves * rank * (leaf_size + rank),
            transcendentals=0,
        ),
    )(place, vectors, leaf_basis, leaf_transfer, upper_transfer, upper_transfer)


def features(x, target):
    row = lax.broadcasted_iota(jnp.int32, x.shape, 0)
    norm = jnp.sum(x * x, axis=0, keepdims=True)
    high, middle, low = thirds(jnp.where(row < 3, x, norm))
    norm_row, one_row, factor = (4, 3, -2.0) if target else (3, 4, 1.0)

    def group(coordinates, norms):
        out = jnp.where(row < 3, coordinates * factor, 0.0)
        if norms is not None:
            out = jnp.where(row == norm_row, norms, jnp.where(row == one_row, 1.0, out))
        return out

    if target:
        groups = [group(high, high), group(middle, middle), group(high, low)]
        groups += [group(low, None), group(middle, None), group(high, None)]
    else:
        groups = [group(high, high), group(middle, middle), group(low, low)]
        groups += [group(high, None), group(high, None), group(middle, None)]
    groups += [jnp.zeros_like(x)] * (DEPTH // 8 - 6)
    return jnp.concatenate(groups, axis=0)


def matern(dist_sq):
    nt = -LOG2E - dist_sq * lax.rsqrt(dist_sq)
    return nt * jnp.exp2(nt)


def near_core(inputs, out_ref, scratch, *, lo, hi, base, leaf_size):
    first_ref, offset_ref, points_ref, vectors_ref, before_p, before_v, after_p, after_v = inputs
    wide_scr, x_scr, a_scr, v_scr, b0, b1, u_scr, kh_scr, kl_scr, item_g, item_h = scratch
    slots, leaves = offset_ref.shape
    first = first_ref[0]
    row8 = lax.broadcasted_iota(jnp.int32, (8, leaf_size), 0)

    wide_scr[...] = jnp.zeros_like(wide_scr)

    def prepare(p_ref, v_ref, start, stop, origin):
        def turn(h, _):
            at = pl.ds(pl.multiple_of((h - origin) * leaf_size, leaf_size), leaf_size)
            to = h + HALO - lo
            centre = (first + h).astype(F32) * 0.5 + 0.5
            wide_scr[0:3] = p_ref[:, at]
            shift = jnp.where(row8 == 0, centre, 0.5)
            scale = jnp.where(row8 == 0, FACTOR[0], FACTOR[1])
            x = jnp.where(row8 < 3, (wide_scr[...] - shift) * scale, 0.0)
            x_scr[to] = x
            a_scr[to] = features(x, False).T.astype(BF16)
            v_high, v_low = halves(v_ref[:, at])
            v_scr[to, 0:16] = jnp.concatenate([v_high, v_low], axis=0)
            v_scr[to, 16:32] = jnp.concatenate([v_high, jnp.zeros_like(v_high)], axis=0)
            return 0

        lax.fori_loop(start, stop, turn, 0)

    if lo < HALO:
        prepare(before_p, before_v, -HALO, 0, -HALO)
    prepare(points_ref, vectors_ref, max(lo - HALO, 0), min(hi + HALO, leaves), 0)
    if hi > leaves - HALO:
        prepare(after_p, after_v, leaves, leaves + HALO, leaves)

    def listing(g, n):
        at = pl.ds(pl.multiple_of(g * leaf_size, leaf_size), leaf_size)
        to = pl.ds(pl.multiple_of((g - base) * leaf_size, leaf_size), leaf_size)
        out_ref[:, to] = NUGGET * vectors_ref[:, at]
        item_g[n] = g - lo
        item_h[n] = g - lo + HALO
        n = n + 1
        for j in range(slots):
            offset = offset_ref[j, g]
            item_g[n] = g - lo
            item_h[n] = g - lo + HALO + offset
            n = n + jnp.where(offset != 0, 1, 0)
        return n

    count = lax.fori_loop(lo, hi, listing, 0)

    def target_features(i, b_scr):
        i = jnp.minimum(i, count - 1)
        g, h = item_g[i], item_h[i]
        apart = (g + HALO - h).astype(F32) * (0.5 * FACTOR[0])
        x = x_scr[g + HALO]
        b_scr[...] = features(jnp.where(row8 == 0, x + apart, x), True).astype(BF16)

    def distances(i, b_scr, c, size):
        h = item_h[jnp.minimum(i, count - 1)]
        dist_sq = jnp.dot(a_scr[h, c : c + size], b_scr[...], preferred_element_type=F32)
        u_scr[c : c + size] = jnp.maximum(dist_sq, TINY)

    def turn(i, b_next, b_later):
        now = jnp.minimum(i, count - 1)
        h = item_h[now]
        acc = jnp.zeros((16, leaf_size), F32)
        size = CHUNK
        for c in range(0, leaf_size, size):
            for r in range(c, c + size, 32):
                high, low = halves(matern(u_scr[r : r + 32]))
                kh_scr[r : r + 32] = high
                kl_scr[r : r + 32] = low
            distances(i + 1, b_next, c, size)
            acc += jnp.dot(v_scr[h, 0:16, c : c + size], kh_scr[c : c + size], preferred_element_type=F32)
            acc += jnp.dot(v_scr[h, 16:32, c : c + size], kl_scr[c : c + size], preferred_element_type=F32)
        target_features(i + 2, b_later)
        done = jnp.where(i < count, (acc[0:8] + acc[8:16]) * GAIN, 0.0)
        at = pl.ds(pl.multiple_of((item_g[now] + (lo - base)) * leaf_size, leaf_size), leaf_size)
        out_ref[:, at] += done

    target_features(0, b0)
    target_features(1, b1)
    distances(0, b0, 0, leaf_size)

    def turns(i, _):
        for j in range(0, UNROLL, 2):
            turn(UNROLL * i + j, b1, b0)
            turn(UNROLL * i + j + 1, b0, b1)
        return 0

    lax.fori_loop(0, (count + (UNROLL - 1)) >> UNROLL.bit_length() - 1, turns, 0)


def near_scratch(count, slots, leaf_size):
    square = (leaf_size, leaf_size)
    leaves = count + 2 * HALO
    return [
        pltpu.VMEM((8, leaf_size), F32),
        pltpu.VMEM((leaves, 8, leaf_size), F32),
        pltpu.VMEM((leaves, leaf_size, DEPTH), BF16),
        pltpu.VMEM((leaves, 32, leaf_size), BF16),
        pltpu.VMEM((DEPTH, leaf_size), BF16),
        pltpu.VMEM((DEPTH, leaf_size), BF16),
        pltpu.VMEM(square, F32),
        pltpu.VMEM(square, BF16),
        pltpu.VMEM(square, BF16),
        pltpu.SMEM((count * (slots + 1) + 8,), jnp.int32),
        pltpu.SMEM((count * (slots + 1) + 8,), jnp.int32),
    ]


NEAR_INPUTS = 8


def near_kernel(*refs, lo, hi, leaf_size):
    near_core(refs[:NEAR_INPUTS], refs[NEAR_INPUTS], refs[NEAR_INPUTS + 1 :], lo=lo, hi=hi, base=lo, leaf_size=leaf_size)


def near_cost(count, leaves, leaf_size):
    return pl.CostEstimate(
        flops=count * 3 * leaf_size * leaf_size * 512,
        bytes_accessed=8 * 11 * leaves * leaf_size,
        transcendentals=count * 6 * leaf_size * leaf_size,
    )


def near_specs():
    return [pl.BlockSpec(memory_space=pltpu.SMEM)] * 2 + [pl.BlockSpec(memory_space=pltpu.VMEM)] * 6


def near_field(inputs, lo, hi):
    slots, leaves = inputs[1].shape
    columns, points = inputs[3].shape
    leaf_size = points // leaves
    return pl.pallas_call(
        functools.partial(near_kernel, lo=lo, hi=hi, leaf_size=leaf_size),
        in_specs=near_specs(),
        out_specs=pl.BlockSpec(memory_space=pltpu.VMEM),
        out_shape=jax.ShapeDtypeStruct((columns, (hi - lo) * leaf_size), F32),
        scratch_shapes=near_scratch(hi - lo, slots, leaf_size),
        compiler_params=pltpu.CompilerParams(vmem_limit_bytes=NEAR_LIMIT),
        cost_estimate=near_cost(hi - lo, leaves, leaf_size),
    )(*inputs)


def last_kernel(*refs, lo, leaf_size):
    inputs = refs[:NEAR_INPUTS]
    done_ref, place_ref, target_ref, source_ref, level0, level1, level2, *hbm, out_ref = refs[NEAR_INPUTS : NEAR_INPUTS + 14]
    coef, coupling, transfer, basis, down, across, local_scr, sems, *scratch = refs[NEAR_INPUTS + 14 :]
    held = (coef, coupling, transfer, basis, down, across)
    peers, slots, _, _ = coupling.shape
    leaves = basis.shape[0]
    parts = sems.shape[1]

    def copies():
        for i, (source, target) in enumerate(zip(hbm, held, strict=True)):
            number = math.gcd(parts, source.shape[0])
            size = source.shape[0] // number
            for j in range(number):
                at = pl.ds(j * size, size)
                yield pltpu.make_async_copy(source.at[at], target.at[at], sems.at[i, j])

    for copy in copies():
        copy.start()

    out_ref[:, 0 : lo * leaf_size] = done_ref[...]
    local_scr[...] = jnp.zeros_like(local_scr)
    near_core(inputs, out_ref, scratch, lo=lo, hi=leaves, base=0, leaf_size=leaf_size)

    for copy in copies():
        copy.wait()

    here = place_ref[0]
    region = dot_plain(level2[2], across[12 + (here >> 2)])
    region = dot_plain(level1[1], across[8 + (here >> 1)]) + dot_turned(region, down[8 + (here >> 1)])
    region = dot_plain(level0[0], across[here]) + dot_turned(region, down[here])

    def far(p, _):
        products = [dot_plain(coef[p, source_ref[k, p]], coupling[p, k]) for k in range(slots)]
        for k in range(slots):
            local_scr[target_ref[k, p]] += products[k]
        return 0

    lax.fori_loop(0, peers, far, 0)

    group = 4

    def back(i, _):
        locals_ = [local_scr[i * group + j] + dot_turned(region, transfer[i * group + j]) for j in range(group)]
        for j in range(group):
            at = pl.ds(pl.multiple_of((i * group + j) * leaf_size, leaf_size), leaf_size)
            out_ref[:, at] += dot_turned(locals_[j], basis[i * group + j])
        return 0

    lax.fori_loop(0, leaves // group, back, 0)


def last_field(inputs, done, place, targets, sources, levels, coefs, far_coupling, leaf_transfer, leaf_basis, upper_transfer, upper_coupling):
    leaves, leaf_size, rank = leaf_basis.shape
    columns, points = inputs[3].shape
    slots = inputs[1].shape[0]
    lo = done.shape[1] // leaf_size
    smem, vmem = pl.BlockSpec(memory_space=pltpu.SMEM), pl.BlockSpec(memory_space=pltpu.VMEM)
    hbm = pl.BlockSpec(memory_space=pl.ANY)
    streamed = (coefs, far_coupling, leaf_transfer, leaf_basis, upper_transfer, upper_coupling)
    return pl.pallas_call(
        functools.partial(last_kernel, lo=lo, leaf_size=leaf_size),
        in_specs=near_specs() + [vmem, smem, smem, smem, vmem, vmem, vmem] + [hbm] * len(streamed),
        out_specs=vmem,
        out_shape=jax.ShapeDtypeStruct((columns, points), F32),
        scratch_shapes=[pltpu.VMEM(x.shape, F32) for x in streamed]
        + [pltpu.VMEM((leaves + 1, columns, rank), F32), pltpu.SemaphoreType.DMA((len(streamed), 8))]
        + near_scratch(leaves - lo, slots, leaf_size),
        compiler_params=pltpu.CompilerParams(vmem_limit_bytes=LAST_LIMIT),
        cost_estimate=near_cost(leaves - lo, leaves, leaf_size),
    )(*inputs, done, place, targets, sources, *levels, *streamed)


def neighbours(points, vectors, width):
    axes = ("leaf", "top")
    count = lax.axis_size("leaf") * lax.axis_size("top")
    head, tail = (jnp.concatenate([points[:, s], vectors[:, s]], axis=0) for s in (slice(0, width), slice(-width, None)))
    before = lax.ppermute(tail, axes, [(i, i + 1) for i in range(count - 1)])
    after = lax.ppermute(head, axes, [(i + 1, i) for i in range(count - 1)])
    return (before[:3], before[3:]), (after[:3], after[3:])


def siblings(sums):
    count = lax.axis_size("leaf")

    def from_partner(x, distance):
        return lax.ppermute(x, "leaf", [(i, i ^ distance) for i in range(count)])

    first = from_partner(sums, 1)
    second = from_partner(sums + first, 2)
    return first, second, from_partner(sums + first + second, 4)


def shards(
    points,
    vectors,
    near_offset,
    leaf_basis,
    leaf_transfer,
    far_target,
    far_source,
    far_coupling,
    upper_transfer,
    upper_coupling,
):
    leaves, leaf_size, _ = leaf_basis.shape
    peers = lax.axis_size("top")
    region, peer = lax.axis_index("leaf"), lax.axis_index("top")
    place = region.astype(jnp.int32).reshape(1)
    first = ((region * peers + peer) * leaves).astype(jnp.int32).reshape(1)

    coefs = coefficients(place, vectors, leaf_basis, leaf_transfer, upper_transfer)
    gathered = lax.all_gather(coefs, "top", axis=0)
    before, after = neighbours(points, vectors, HALO * leaf_size)
    inputs = (first, near_offset.T, points, vectors, *before, *after)
    early = near_field(inputs, 0, EARLY_LEAVES)
    gathered, early = lax.optimization_barrier((gathered, early))
    levels = siblings(jnp.sum(gathered[:, leaves:], axis=0))
    return last_field(
        inputs,
        early,
        place,
        far_target[0].T,
        far_source[0].T,
        levels,
        gathered,
        far_coupling[0],
        leaf_transfer,
        leaf_basis,
        upper_transfer,
        upper_coupling,
    )


def solution(mesh):
    split = ("leaf", "top")
    in_specs = (
        P(None, split),
        P(None, split),
        P(split, None),
        P(split, None, None),
        P(split, None, None),
        P(split, None, None),
        P(split, None, None),
        P(split, None, None, None, None),
        P(),
        P(),
    )
    return jax.shard_map(shards, mesh=mesh, in_specs=in_specs, out_specs=P(None, split), check_vma=False)
```

```python
import functools
import math

import jax
import jax.numpy as jnp
from jax import lax
from jax.experimental import pallas as pl
from jax.experimental.pallas import tpu as pltpu
from jax.sharding import PartitionSpec as P

F32, BF16 = jnp.float32, jnp.bfloat16
NUGGET = 0.1
SCALES = (0.3, 0.15, 0.15)
LOG2E = math.log2(math.e)
FACTOR = tuple(math.sqrt(3.0) * LOG2E / scale for scale in SCALES)
GAIN = -0.25 * math.log(2.0) * math.e
TINY = 1e-20
DEPTH = 64
HALO = 2
CHUNK = 64
UNROLL = 4
NEAR_LIMIT = 20 << 20
WIDE_LIMIT = 56 << 20
LAST_LIMIT = 56 << 20


def halves(x):
    high = x.astype(BF16)
    return high, (x - high.astype(F32)).astype(BF16)


def thirds(x):
    high = x.astype(BF16).astype(F32)
    rest = x - high
    middle = rest.astype(BF16).astype(F32)
    return high, middle, rest - middle


def dot_plain(x, matrix):
    n = matrix.shape[1]
    left = jnp.concatenate(halves(x), axis=0)
    out = jnp.dot(left, jnp.concatenate(halves(matrix), axis=1), preferred_element_type=F32)
    return out[0:8, 0:n] + out[8:16, 0:n] + out[0:8, n : 2 * n]


def dot_turned(x, matrix):
    high, low = halves(x)
    upper = jnp.concatenate([high, high], axis=1)
    lower = jnp.concatenate([low, jnp.zeros_like(low)], axis=1)
    out = lax.dot_general(
        jnp.concatenate([upper, lower], axis=0),
        jnp.concatenate(halves(matrix), axis=1),
        (((1,), (1,)), ((), ())),
        preferred_element_type=F32,
    )
    return out[0:8] + out[8:16]


def coef_kernel(place_ref, vec_hbm, basis_hbm, transfer_hbm, up0_ref, up1_ref, coef_ref, vec, basis, transfer, sems, *, group):
    del place_ref
    leaves, leaf_size, _ = basis.shape
    groups = leaves // group

    def copies(i):
        at = pl.ds(i * group, group)
        points = pl.ds(pl.multiple_of(i * (group * leaf_size), group * leaf_size), group * leaf_size)
        return (
            pltpu.make_async_copy(vec_hbm.at[:, points], vec.at[:, points], sems.at[0, i]),
            pltpu.make_async_copy(basis_hbm.at[at], basis.at[at], sems.at[1, i]),
            pltpu.make_async_copy(transfer_hbm.at[at], transfer.at[at], sems.at[2, i]),
        )

    for i in range(groups):
        for copy in copies(i):
            copy.start()

    def turn(i, total):
        for copy in copies(i):
            copy.wait()
        coefs = []
        for j in range(group):
            at = pl.ds(pl.multiple_of((i * group + j) * leaf_size, leaf_size), leaf_size)
            coefs.append(dot_plain(vec[:, at], basis[i * group + j]))
        for j in range(group):
            coef_ref[i * group + j] = coefs[j]
            total += dot_plain(coefs[j], transfer[i * group + j])
        return total

    part = lax.fori_loop(0, groups, turn, jnp.zeros(coef_ref.shape[1:], F32))
    coef_ref[leaves] = part
    part = dot_plain(part, up0_ref[0])
    coef_ref[leaves + 1] = part
    coef_ref[leaves + 2] = dot_plain(part, up1_ref[0])


def coefficients(place, vectors, leaf_basis, leaf_transfer, upper_transfer):
    leaves, leaf_size, rank = leaf_basis.shape
    columns = vectors.shape[0]
    group = 4
    node = (1, rank, rank)
    hbm = pl.BlockSpec(memory_space=pl.ANY)
    return pl.pallas_call(
        functools.partial(coef_kernel, group=group),
        grid_spec=pltpu.PrefetchScalarGridSpec(
            num_scalar_prefetch=1,
            grid=(1,),
            in_specs=[
                hbm,
                hbm,
                hbm,
                pl.BlockSpec(node, lambda i, p: (p[0], 0, 0)),
                pl.BlockSpec(node, lambda i, p: (8 + (p[0] >> 1), 0, 0)),
            ],
            out_specs=pl.BlockSpec((leaves + 3, columns, rank), lambda i, p: (0, 0, 0)),
            scratch_shapes=[
                pltpu.VMEM(vectors.shape, F32),
                pltpu.VMEM(leaf_basis.shape, F32),
                pltpu.VMEM(leaf_transfer.shape, F32),
                pltpu.SemaphoreType.DMA((3, leaves // group)),
            ],
        ),
        out_shape=jax.ShapeDtypeStruct((leaves + 3, columns, rank), F32),
        compiler_params=pltpu.CompilerParams(vmem_limit_bytes=WIDE_LIMIT),
        cost_estimate=pl.CostEstimate(
            flops=leaves * 16 * rank * (leaf_size + rank) * 4,
            bytes_accessed=4 * leaves * rank * (leaf_size + rank),
            transcendentals=0,
        ),
    )(place, vectors, leaf_basis, leaf_transfer, upper_transfer, upper_transfer)


def features(x, target):
    row = lax.broadcasted_iota(jnp.int32, x.shape, 0)
    norm = jnp.sum(x * x, axis=0, keepdims=True)
    if target:
        high, middle, low = thirds(jnp.where(row < 3, -2.0 * x, norm))
        groups = [jnp.where(row == 3, 1.0, high), jnp.where(row == 3, 1.0, middle)]
        groups += [jnp.where(row == 3, 1.0, jnp.where(row < 3, high, low)), low, middle, high]
    else:
        high, middle, low = thirds(jnp.where(row < 4, jnp.where(row < 3, x, norm), 0.0))
        one = jnp.where(row == 4, 1.0, 0.0)
        groups = [high + one, middle + one, low + one]
        groups += [jnp.where(row < 3, high, 0.0), jnp.where(row < 3, high, 0.0), jnp.where(row < 3, middle, 0.0)]
    groups += [jnp.zeros_like(x)] * (DEPTH // 8 - 6)
    return jnp.concatenate(groups, axis=0)


def matern(dist_sq):
    nt = -LOG2E - dist_sq * lax.rsqrt(dist_sq)
    return nt * jnp.exp2(nt)


def near_core(inputs, out_ref, scratch, *, begin, stop, leaf_size):
    first_ref, offset_ref, points_ref, vectors_ref, before_p, before_v, after_p, after_v = inputs
    wide_scr, x_scr, a_scr, v_scr, b0, b1, u_scr, kh_scr, kl_scr, item_g, item_h = scratch
    slots, leaves = offset_ref.shape
    first = first_ref[0]
    row8 = lax.broadcasted_iota(jnp.int32, (8, leaf_size), 0)

    wide_scr[...] = jnp.zeros_like(wide_scr)

    def listing(g, n):
        item_g[n] = g
        item_h[n] = g + HALO
        n = n + 1
        for j in range(slots):
            offset = offset_ref[j, g]
            item_g[n] = g
            item_h[n] = g + HALO + offset
            n = n + jnp.where(offset != 0, 1, 0)
        return n

    count = lax.fori_loop(0, leaves, listing, 0)
    end = count if stop is None else jnp.minimum(stop, count)
    g_first = item_g[jnp.minimum(begin, count - 1)]
    g_last = item_g[end - 1]

    def prepare(p_ref, v_ref, start, stop, origin):
        def turn(h, _):
            at = pl.ds(pl.multiple_of((h - origin) * leaf_size, leaf_size), leaf_size)
            to = h + HALO
            centre = (first + h).astype(F32) * 0.5 + 0.5
            wide_scr[0:3] = p_ref[:, at]
            shift = jnp.where(row8 == 0, centre, 0.5)
            scale = jnp.where(row8 == 0, FACTOR[0], FACTOR[1])
            x = jnp.where(row8 < 3, (wide_scr[...] - shift) * scale, 0.0)
            x_scr[to] = x
            a_scr[to] = features(x, False).T.astype(BF16)
            v_high, v_low = halves(v_ref[:, at])
            v_scr[to, 0:16] = jnp.concatenate([v_high, v_low], axis=0)
            v_scr[to, 16:32] = jnp.concatenate([v_high, jnp.zeros_like(v_high)], axis=0)
            return 0

        lax.fori_loop(start, stop, turn, 0)

    prepare(before_p, before_v, jnp.minimum(g_first - HALO, 0), 0, -HALO)
    prepare(points_ref, vectors_ref, jnp.maximum(g_first - HALO, 0), jnp.minimum(g_last + HALO + 1, leaves), 0)
    prepare(after_p, after_v, leaves, jnp.maximum(g_last + HALO + 1, leaves), leaves)

    def target_features(i, b_scr):
        i = jnp.minimum(i, count - 1)
        g, h = item_g[i], item_h[i]
        apart = (g + HALO - h).astype(F32) * (0.5 * FACTOR[0])
        x = x_scr[g + HALO]
        b_scr[...] = features(jnp.where(row8 == 0, x + apart, x), True).astype(BF16)

    def distances(i, b_scr, c, size):
        h = item_h[jnp.minimum(i, count - 1)]
        dist_sq = jnp.dot(a_scr[h, c : c + size], b_scr[...], preferred_element_type=F32)
        u_scr[c : c + size] = jnp.maximum(dist_sq, TINY)

    def turn(i, b_next, b_later):
        now = jnp.minimum(i, count - 1)
        h = item_h[now]
        acc = jnp.zeros((16, leaf_size), F32)
        size = CHUNK
        for c in range(0, leaf_size, size):
            for r in range(c, c + size, 32):
                high, low = halves(matern(u_scr[r : r + 32]))
                kh_scr[r : r + 32] = high
                kl_scr[r : r + 32] = low
            distances(i + 1, b_next, c, size)
            acc += jnp.dot(v_scr[h, 0:16, c : c + size], kh_scr[c : c + size], preferred_element_type=F32)
            acc += jnp.dot(v_scr[h, 16:32, c : c + size], kl_scr[c : c + size], preferred_element_type=F32)
        target_features(i + 2, b_later)
        done = jnp.where(i < end, (acc[0:8] + acc[8:16]) * GAIN, 0.0)
        at = pl.ds(pl.multiple_of(item_g[now] * leaf_size, leaf_size), leaf_size)
        out_ref[:, at] += done

    target_features(begin, b0)
    target_features(begin + 1, b1)
    distances(begin, b0, 0, leaf_size)

    def turns(i, _):
        for j in range(0, UNROLL, 2):
            turn(begin + UNROLL * i + j, b1, b0)
            turn(begin + UNROLL * i + j + 1, b0, b1)
        return 0

    lax.fori_loop(0, jnp.maximum(end - begin + (UNROLL - 1), 0) >> UNROLL.bit_length() - 1, turns, 0)


def near_scratch(count, slots, leaf_size):
    square = (leaf_size, leaf_size)
    leaves = count + 2 * HALO
    return [
        pltpu.VMEM((8, leaf_size), F32),
        pltpu.VMEM((leaves, 8, leaf_size), F32),
        pltpu.VMEM((leaves, leaf_size, DEPTH), BF16),
        pltpu.VMEM((leaves, 32, leaf_size), BF16),
        pltpu.VMEM((DEPTH, leaf_size), BF16),
        pltpu.VMEM((DEPTH, leaf_size), BF16),
        pltpu.VMEM(square, F32),
        pltpu.VMEM(square, BF16),
        pltpu.VMEM(square, BF16),
        pltpu.SMEM((count * (slots + 1) + 8,), jnp.int32),
        pltpu.SMEM((count * (slots + 1) + 8,), jnp.int32),
    ]


NEAR_INPUTS = 8


def near_kernel(*refs, stop, leaf_size):
    inputs, out_ref = refs[:NEAR_INPUTS], refs[NEAR_INPUTS]
    out_ref[...] = NUGGET * inputs[3][...]
    near_core(inputs, out_ref, refs[NEAR_INPUTS + 1 :], begin=0, stop=stop, leaf_size=leaf_size)


def near_cost(blocks, leaves, leaf_size):
    return pl.CostEstimate(
        flops=blocks * leaf_size * leaf_size * 512,
        bytes_accessed=8 * 11 * leaves * leaf_size,
        transcendentals=blocks * 2 * leaf_size * leaf_size,
    )


def near_specs():
    return [pl.BlockSpec(memory_space=pltpu.SMEM)] * 2 + [pl.BlockSpec(memory_space=pltpu.VMEM)] * 6


def near_field(inputs, stop):
    slots, leaves = inputs[1].shape
    columns, points = inputs[3].shape
    leaf_size = points // leaves
    return pl.pallas_call(
        functools.partial(near_kernel, stop=stop, leaf_size=leaf_size),
        in_specs=near_specs(),
        out_specs=pl.BlockSpec(memory_space=pltpu.VMEM),
        out_shape=jax.ShapeDtypeStruct((columns, points), F32),
        scratch_shapes=near_scratch(leaves, slots, leaf_size),
        compiler_params=pltpu.CompilerParams(vmem_limit_bytes=NEAR_LIMIT),
        cost_estimate=near_cost(stop, leaves, leaf_size),
    )(*inputs)


def last_kernel(*refs, begin, leaf_size):
    inputs = refs[:NEAR_INPUTS]
    done_ref, place_ref, target_ref, source_ref, level0, level1, level2, *hbm, out_ref = refs[NEAR_INPUTS : NEAR_INPUTS + 14]
    coef, coupling, transfer, basis, down, across, local_scr, sems, *scratch = refs[NEAR_INPUTS + 14 :]
    held = (coef, coupling, transfer, basis, down, across)
    peers, slots, _, _ = coupling.shape
    leaves = basis.shape[0]
    parts = sems.shape[1]

    def copies():
        for i, (source, target) in enumerate(zip(hbm, held, strict=True)):
            number = math.gcd(parts, source.shape[0])
            size = source.shape[0] // number
            for j in range(number):
                at = pl.ds(j * size, size)
                yield pltpu.make_async_copy(source.at[at], target.at[at], sems.at[i, j])

    for copy in copies():
        copy.start()

    out_ref[...] = done_ref[...]
    local_scr[...] = jnp.zeros_like(local_scr)
    near_core(inputs, out_ref, scratch, begin=begin, stop=None, leaf_size=leaf_size)

    for copy in copies():
        copy.wait()

    here = place_ref[0]
    region = dot_plain(level2[2], across[12 + (here >> 2)])
    region = dot_plain(level1[1], across[8 + (here >> 1)]) + dot_turned(region, down[8 + (here >> 1)])
    region = dot_plain(level0[0], across[here]) + dot_turned(region, down[here])

    def far(p, _):
        products = [dot_plain(coef[p, source_ref[k, p]], coupling[p, k]) for k in range(slots)]
        for k in range(slots):
            local_scr[target_ref[k, p]] += products[k]
        return 0

    lax.fori_loop(0, peers, far, 0)

    group = 4

    def back(i, _):
        locals_ = [local_scr[i * group + j] + dot_turned(region, transfer[i * group + j]) for j in range(group)]
        for j in range(group):
            at = pl.ds(pl.multiple_of((i * group + j) * leaf_size, leaf_size), leaf_size)
            out_ref[:, at] += dot_turned(locals_[j], basis[i * group + j])
        return 0

    lax.fori_loop(0, leaves // group, back, 0)


def last_field(inputs, begin, done, place, targets, sources, levels, coefs, far_coupling, leaf_transfer, leaf_basis, upper_transfer, upper_coupling):
    leaves, leaf_size, rank = leaf_basis.shape
    columns, points = inputs[3].shape
    slots = inputs[1].shape[0]
    smem, vmem = pl.BlockSpec(memory_space=pltpu.SMEM), pl.BlockSpec(memory_space=pltpu.VMEM)
    hbm = pl.BlockSpec(memory_space=pl.ANY)
    streamed = (coefs, far_coupling, leaf_transfer, leaf_basis, upper_transfer, upper_coupling)
    return pl.pallas_call(
        functools.partial(last_kernel, begin=begin, leaf_size=leaf_size),
        in_specs=near_specs() + [vmem, smem, smem, smem, vmem, vmem, vmem] + [hbm] * len(streamed),
        out_specs=vmem,
        out_shape=jax.ShapeDtypeStruct((columns, points), F32),
        scratch_shapes=[pltpu.VMEM(x.shape, F32) for x in streamed]
        + [pltpu.VMEM((leaves + 1, columns, rank), F32), pltpu.SemaphoreType.DMA((len(streamed), 8))]
        + near_scratch(leaves, slots, leaf_size),
        compiler_params=pltpu.CompilerParams(vmem_limit_bytes=LAST_LIMIT),
        cost_estimate=near_cost(leaves, leaves, leaf_size),
    )(*inputs, done, place, targets, sources, *levels, *streamed)


def neighbours(points, vectors, width):
    axes = ("leaf", "top")
    count = lax.axis_size("leaf") * lax.axis_size("top")
    head, tail = (jnp.concatenate([points[:, s], vectors[:, s]], axis=0) for s in (slice(0, width), slice(-width, None)))
    before = lax.ppermute(tail, axes, [(i, i + 1) for i in range(count - 1)])
    after = lax.ppermute(head, axes, [(i + 1, i) for i in range(count - 1)])
    return (before[:3], before[3:]), (after[:3], after[3:])


def siblings(sums):
    count = lax.axis_size("leaf")

    def from_partner(x, distance):
        return lax.ppermute(x, "leaf", [(i, i ^ distance) for i in range(count)])

    first = from_partner(sums, 1)
    second = from_partner(sums + first, 2)
    return first, second, from_partner(sums + first + second, 4)


def shards(
    points,
    vectors,
    near_offset,
    leaf_basis,
    leaf_transfer,
    far_target,
    far_source,
    far_coupling,
    upper_transfer,
    upper_coupling,
):
    leaves, leaf_size, _ = leaf_basis.shape
    peers = lax.axis_size("top")
    region, peer = lax.axis_index("leaf"), lax.axis_index("top")
    place = region.astype(jnp.int32).reshape(1)
    first = ((region * peers + peer) * leaves).astype(jnp.int32).reshape(1)

    coefs = coefficients(place, vectors, leaf_basis, leaf_transfer, upper_transfer)
    gathered = lax.all_gather(coefs, "top", axis=0)
    before, after = neighbours(points, vectors, HALO * leaf_size)
    inputs = (first, near_offset.T, points, vectors, *before, *after)
    early_blocks = 2 * leaves
    early = near_field(inputs, early_blocks)
    gathered, early = lax.optimization_barrier((gathered, early))
    levels = siblings(jnp.sum(gathered[:, leaves:], axis=0))
    return last_field(
        inputs,
        early_blocks,
        early,
        place,
        far_target[0].T,
        far_source[0].T,
        levels,
        gathered,
        far_coupling[0],
        leaf_transfer,
        leaf_basis,
        upper_transfer,
        upper_coupling,
    )


def solution(mesh):
    split = ("leaf", "top")
    in_specs = (
        P(None, split),
        P(None, split),
        P(split, None),
        P(split, None, None),
        P(split, None, None),
        P(split, None, None),
        P(split, None, None),
        P(split, None, None, None, None),
        P(),
        P(),
    )
    return jax.shard_map(shards, mesh=mesh, in_specs=in_specs, out_specs=P(None, split), check_vma=False)
```

```python
import functools
import math

import jax
import jax.numpy as jnp
from jax import lax
from jax.experimental import pallas as pl
from jax.experimental.pallas import tpu as pltpu
from jax.sharding import PartitionSpec as P

F32, BF16 = jnp.float32, jnp.bfloat16
NUGGET = 0.1
SCALES = (0.3, 0.15, 0.15)
LOG2E = math.log2(math.e)
FACTOR = tuple(math.sqrt(3.0) * LOG2E / scale for scale in SCALES)
GAIN = -0.25 * math.log(2.0) * math.e
TINY = 1e-20
DEPTH = 64
HALO = 2
CHUNK = 64
UNROLL = 4
NEAR_LIMIT = 20 << 20
WIDE_LIMIT = 56 << 20
LAST_LIMIT = 56 << 20


def halves(x):
    high = x.astype(BF16)
    return high, (x - high.astype(F32)).astype(BF16)


def thirds(x):
    high = x.astype(BF16).astype(F32)
    rest = x - high
    middle = rest.astype(BF16).astype(F32)
    return high, middle, rest - middle


def dot_plain(x, matrix):
    n = matrix.shape[1]
    left = jnp.concatenate(halves(x), axis=0)
    out = jnp.dot(left, jnp.concatenate(halves(matrix), axis=1), preferred_element_type=F32)
    return out[0:8, 0:n] + out[8:16, 0:n] + out[0:8, n : 2 * n]


def dot_turned(x, matrix):
    high, low = halves(x)
    upper = jnp.concatenate([high, high], axis=1)
    lower = jnp.concatenate([low, jnp.zeros_like(low)], axis=1)
    out = lax.dot_general(
        jnp.concatenate([upper, lower], axis=0),
        jnp.concatenate(halves(matrix), axis=1),
        (((1,), (1,)), ((), ())),
        preferred_element_type=F32,
    )
    return out[0:8] + out[8:16]


def coef_kernel(place_ref, vec_hbm, basis_hbm, transfer_hbm, up0_ref, up1_ref, coef_ref, vec, basis, transfer, sems, *, group):
    del place_ref
    leaves, leaf_size, _ = basis.shape
    groups = leaves // group

    def copies(i):
        at = pl.ds(i * group, group)
        points = pl.ds(pl.multiple_of(i * (group * leaf_size), group * leaf_size), group * leaf_size)
        return (
            pltpu.make_async_copy(vec_hbm.at[:, points], vec.at[:, points], sems.at[0, i]),
            pltpu.make_async_copy(basis_hbm.at[at], basis.at[at], sems.at[1, i]),
            pltpu.make_async_copy(transfer_hbm.at[at], transfer.at[at], sems.at[2, i]),
        )

    for i in range(groups):
        for copy in copies(i):
            copy.start()

    def turn(i, total):
        for copy in copies(i):
            copy.wait()
        coefs = []
        for j in range(group):
            at = pl.ds(pl.multiple_of((i * group + j) * leaf_size, leaf_size), leaf_size)
            coefs.append(dot_plain(vec[:, at], basis[i * group + j]))
        for j in range(group):
            coef_ref[i * group + j] = coefs[j]
            total += dot_plain(coefs[j], transfer[i * group + j])
        return total

    part = lax.fori_loop(0, groups, turn, jnp.zeros(coef_ref.shape[1:], F32))
    coef_ref[leaves] = part
    part = dot_plain(part, up0_ref[0])
    coef_ref[leaves + 1] = part
    coef_ref[leaves + 2] = dot_plain(part, up1_ref[0])


def coefficients(place, vectors, leaf_basis, leaf_transfer, upper_transfer):
    leaves, leaf_size, rank = leaf_basis.shape
    columns = vectors.shape[0]
    group = 4
    node = (1, rank, rank)
    hbm = pl.BlockSpec(memory_space=pl.ANY)
    return pl.pallas_call(
        functools.partial(coef_kernel, group=group),
        grid_spec=pltpu.PrefetchScalarGridSpec(
            num_scalar_prefetch=1,
            grid=(1,),
            in_specs=[
                hbm,
                hbm,
                hbm,
                pl.BlockSpec(node, lambda i, p: (p[0], 0, 0)),
                pl.BlockSpec(node, lambda i, p: (8 + (p[0] >> 1), 0, 0)),
            ],
            out_specs=pl.BlockSpec((leaves + 3, columns, rank), lambda i, p: (0, 0, 0)),
            scratch_shapes=[
                pltpu.VMEM(vectors.shape, F32),
                pltpu.VMEM(leaf_basis.shape, F32),
                pltpu.VMEM(leaf_transfer.shape, F32),
                pltpu.SemaphoreType.DMA((3, leaves // group)),
            ],
        ),
        out_shape=jax.ShapeDtypeStruct((leaves + 3, columns, rank), F32),
        compiler_params=pltpu.CompilerParams(vmem_limit_bytes=WIDE_LIMIT),
        cost_estimate=pl.CostEstimate(
            flops=leaves * 16 * rank * (leaf_size + rank) * 4,
            bytes_accessed=4 * leaves * rank * (leaf_size + rank),
            transcendentals=0,
        ),
    )(place, vectors, leaf_basis, leaf_transfer, upper_transfer, upper_transfer)


def features(x, target):
    row = lax.broadcasted_iota(jnp.int32, x.shape, 0)
    norm = jnp.sum(x * x, axis=0, keepdims=True)
    if target:
        high, middle, low = thirds(jnp.where(row < 3, -2.0 * x, norm))
        groups = [jnp.where(row == 3, 1.0, high), jnp.where(row == 3, 1.0, middle)]
        groups += [jnp.where(row == 3, 1.0, jnp.where(row < 3, high, low)), low, middle, high]
    else:
        high, middle, low = thirds(jnp.where(row < 4, jnp.where(row < 3, x, norm), 0.0))
        one = jnp.where(row == 4, 1.0, 0.0)
        groups = [high + one, middle + one, low + one]
        groups += [jnp.where(row < 3, high, 0.0), jnp.where(row < 3, high, 0.0), jnp.where(row < 3, middle, 0.0)]
    groups += [jnp.zeros_like(x)] * (DEPTH // 8 - 6)
    return jnp.concatenate(groups, axis=0)


def matern(dist_sq):
    nt = -LOG2E - dist_sq * lax.rsqrt(dist_sq)
    return nt * jnp.exp2(nt)


def near_core(inputs, out_ref, scratch, *, begin, stop, leaf_size):
    first_ref, offset_ref, points_ref, vectors_ref, before_p, before_v, after_p, after_v = inputs
    wide_scr, x_scr, a_scr, v_scr, b0, b1, u_scr, kh_scr, kl_scr, item_g, item_h = scratch
    slots, leaves = offset_ref.shape
    first = first_ref[0]
    row8 = lax.broadcasted_iota(jnp.int32, (8, leaf_size), 0)

    wide_scr[...] = jnp.zeros_like(wide_scr)

    def listing(g, n):
        item_g[n] = g
        item_h[n] = g + HALO
        n = n + 1
        for j in range(slots):
            offset = offset_ref[j, g]
            item_g[n] = g
            item_h[n] = g + HALO + offset
            n = n + jnp.where(offset != 0, 1, 0)
        return n

    count = lax.fori_loop(0, leaves, listing, 0)
    end = count if stop is None else jnp.minimum(stop, count)
    g_first = item_g[jnp.minimum(begin, count - 1)]
    g_last = item_g[end - 1]

    def prepare(p_ref, v_ref, start, stop, origin):
        def turn(h, _):
            at = pl.ds(pl.multiple_of((h - origin) * leaf_size, leaf_size), leaf_size)
            to = h + HALO
            centre = (first + h).astype(F32) * 0.5 + 0.5
            wide_scr[0:3] = p_ref[:, at]
            shift = jnp.where(row8 == 0, centre, 0.5)
            scale = jnp.where(row8 == 0, FACTOR[0], FACTOR[1])
            x = jnp.where(row8 < 3, (wide_scr[...] - shift) * scale, 0.0)
            x_scr[to] = x
            a_scr[to] = features(x, False).T.astype(BF16)
            v_high, v_low = halves(v_ref[:, at])
            v_scr[to, 0:16] = jnp.concatenate([v_high, v_low], axis=0)
            v_scr[to, 16:32] = jnp.concatenate([v_high, jnp.zeros_like(v_high)], axis=0)
            return 0

        lax.fori_loop(start, stop, turn, 0)

    prepare(before_p, before_v, jnp.minimum(g_first - HALO, 0), 0, -HALO)
    prepare(points_ref, vectors_ref, jnp.maximum(g_first - HALO, 0), jnp.minimum(g_last + HALO + 1, leaves), 0)
    prepare(after_p, after_v, leaves, jnp.maximum(g_last + HALO + 1, leaves), leaves)

    def target_features(i, b_scr):
        i = jnp.minimum(i, count - 1)
        g, h = item_g[i], item_h[i]
        apart = (g + HALO - h).astype(F32) * (0.5 * FACTOR[0])
        x = x_scr[g + HALO]
        b_scr[...] = features(jnp.where(row8 == 0, x + apart, x), True).astype(BF16)

    def distances(i, b_scr, c, size):
        h = item_h[jnp.minimum(i, count - 1)]
        dist_sq = jnp.dot(a_scr[h, c : c + size], b_scr[...], preferred_element_type=F32)
        u_scr[c : c + size] = jnp.maximum(dist_sq, TINY)

    def turn(i, b_next, b_later):
        now = jnp.minimum(i, count - 1)
        h = item_h[now]
        acc = jnp.zeros((16, leaf_size), F32)
        size = CHUNK
        for c in range(0, leaf_size, size):
            for r in range(c, c + size, 32):
                high, low = halves(matern(u_scr[r : r + 32]))
                kh_scr[r : r + 32] = high
                kl_scr[r : r + 32] = low
            distances(i + 1, b_next, c, size)
            acc += jnp.dot(v_scr[h, 0:16, c : c + size], kh_scr[c : c + size], preferred_element_type=F32)
            acc += jnp.dot(v_scr[h, 16:32, c : c + size], kl_scr[c : c + size], preferred_element_type=F32)
        target_features(i + 2, b_later)
        done = jnp.where(i < end, (acc[0:8] + acc[8:16]) * GAIN, 0.0)
        at = pl.ds(pl.multiple_of(item_g[now] * leaf_size, leaf_size), leaf_size)
        out_ref[:, at] += done

    target_features(begin, b0)
    target_features(begin + 1, b1)
    distances(begin, b0, 0, leaf_size)

    def turns(i, _):
        for j in range(0, UNROLL, 2):
            turn(begin + UNROLL * i + j, b1, b0)
            turn(begin + UNROLL * i + j + 1, b0, b1)
        return 0

    lax.fori_loop(0, jnp.maximum(end - begin + (UNROLL - 1), 0) >> UNROLL.bit_length() - 1, turns, 0)


def near_scratch(count, slots, leaf_size):
    square = (leaf_size, leaf_size)
    leaves = count + 2 * HALO
    return [
        pltpu.VMEM((8, leaf_size), F32),
        pltpu.VMEM((leaves, 8, leaf_size), F32),
        pltpu.VMEM((leaves, leaf_size, DEPTH), BF16),
        pltpu.VMEM((leaves, 32, leaf_size), BF16),
        pltpu.VMEM((DEPTH, leaf_size), BF16),
        pltpu.VMEM((DEPTH, leaf_size), BF16),
        pltpu.VMEM(square, F32),
        pltpu.VMEM(square, BF16),
        pltpu.VMEM(square, BF16),
        pltpu.SMEM((count * (slots + 1) + 8,), jnp.int32),
        pltpu.SMEM((count * (slots + 1) + 8,), jnp.int32),
    ]


NEAR_INPUTS = 8


def near_kernel(*refs, stop, leaf_size):
    inputs, out_ref = refs[:NEAR_INPUTS], refs[NEAR_INPUTS]
    out_ref[...] = NUGGET * inputs[3][...]
    near_core(inputs, out_ref, refs[NEAR_INPUTS + 1 :], begin=0, stop=stop, leaf_size=leaf_size)


def near_cost(blocks, leaves, leaf_size):
    return pl.CostEstimate(
        flops=blocks * leaf_size * leaf_size * 512,
        bytes_accessed=8 * 11 * leaves * leaf_size,
        transcendentals=blocks * 2 * leaf_size * leaf_size,
    )


def near_specs():
    return [pl.BlockSpec(memory_space=pltpu.SMEM)] * 2 + [pl.BlockSpec(memory_space=pltpu.VMEM)] * 6


def near_field(inputs, stop):
    slots, leaves = inputs[1].shape
    columns, points = inputs[3].shape
    leaf_size = points // leaves
    return pl.pallas_call(
        functools.partial(near_kernel, stop=stop, leaf_size=leaf_size),
        in_specs=near_specs(),
        out_specs=pl.BlockSpec(memory_space=pltpu.VMEM),
        out_shape=jax.ShapeDtypeStruct((columns, points), F32),
        scratch_shapes=near_scratch(leaves, slots, leaf_size),
        compiler_params=pltpu.CompilerParams(vmem_limit_bytes=NEAR_LIMIT),
        cost_estimate=near_cost(stop, leaves, leaf_size),
    )(*inputs)


def last_kernel(*refs, begin, leaf_size):
    inputs = refs[:NEAR_INPUTS]
    done_ref, place_ref, target_ref, source_ref, level0, level1, level2, *hbm, out_ref = refs[NEAR_INPUTS : NEAR_INPUTS + 14]
    coef, coupling, transfer, basis, down, across, local_scr, sems, *scratch = refs[NEAR_INPUTS + 14 :]
    held = (coef, coupling, transfer, basis, down, across)
    peers, slots, _, _ = coupling.shape
    leaves = basis.shape[0]
    parts = sems.shape[1]

    def copies():
        for i, (source, target) in enumerate(zip(hbm, held, strict=True)):
            number = math.gcd(parts, source.shape[0])
            size = source.shape[0] // number
            for j in range(number):
                at = pl.ds(j * size, size)
                yield pltpu.make_async_copy(source.at[at], target.at[at], sems.at[i, j])

    for copy in copies():
        copy.start()

    out_ref[...] = done_ref[...]
    local_scr[...] = jnp.zeros_like(local_scr)
    near_core(inputs, out_ref, scratch, begin=begin, stop=None, leaf_size=leaf_size)

    for copy in copies():
        copy.wait()

    here = place_ref[0]
    region = dot_plain(level2[2], across[12 + (here >> 2)])
    region = dot_plain(level1[1], across[8 + (here >> 1)]) + dot_turned(region, down[8 + (here >> 1)])
    region = dot_plain(level0[0], across[here]) + dot_turned(region, down[here])

    def far(p, _):
        products = [dot_plain(coef[p, source_ref[k, p]], coupling[p, k]) for k in range(slots)]
        for k in range(slots):
            local_scr[target_ref[k, p]] += products[k]
        return 0

    lax.fori_loop(0, peers, far, 0, unroll=2)

    group = 8

    def back(i, _):
        locals_ = [local_scr[i * group + j] + dot_turned(region, transfer[i * group + j]) for j in range(group)]
        for j in range(group):
            at = pl.ds(pl.multiple_of((i * group + j) * leaf_size, leaf_size), leaf_size)
            out_ref[:, at] += dot_turned(locals_[j], basis[i * group + j])
        return 0

    lax.fori_loop(0, leaves // group, back, 0)


def last_field(inputs, begin, done, place, targets, sources, levels, coefs, far_coupling, leaf_transfer, leaf_basis, upper_transfer, upper_coupling):
    leaves, leaf_size, rank = leaf_basis.shape
    columns, points = inputs[3].shape
    slots = inputs[1].shape[0]
    smem, vmem = pl.BlockSpec(memory_space=pltpu.SMEM), pl.BlockSpec(memory_space=pltpu.VMEM)
    hbm = pl.BlockSpec(memory_space=pl.ANY)
    streamed = (coefs, far_coupling, leaf_transfer, leaf_basis, upper_transfer, upper_coupling)
    return pl.pallas_call(
        functools.partial(last_kernel, begin=begin, leaf_size=leaf_size),
        in_specs=near_specs() + [vmem, smem, smem, smem, vmem, vmem, vmem] + [hbm] * len(streamed),
        out_specs=vmem,
        out_shape=jax.ShapeDtypeStruct((columns, points), F32),
        scratch_shapes=[pltpu.VMEM(x.shape, F32) for x in streamed]
        + [pltpu.VMEM((leaves + 1, columns, rank), F32), pltpu.SemaphoreType.DMA((len(streamed), 8))]
        + near_scratch(leaves, slots, leaf_size),
        compiler_params=pltpu.CompilerParams(vmem_limit_bytes=LAST_LIMIT),
        cost_estimate=near_cost(leaves, leaves, leaf_size),
    )(*inputs, done, place, targets, sources, *levels, *streamed)


def neighbours(points, vectors, width):
    axes = ("leaf", "top")
    count = lax.axis_size("leaf") * lax.axis_size("top")
    head, tail = (jnp.concatenate([points[:, s], vectors[:, s]], axis=0) for s in (slice(0, width), slice(-width, None)))
    before = lax.ppermute(tail, axes, [(i, i + 1) for i in range(count - 1)])
    after = lax.ppermute(head, axes, [(i + 1, i) for i in range(count - 1)])
    return (before[:3], before[3:]), (after[:3], after[3:])


def siblings(sums):
    count = lax.axis_size("leaf")

    def from_partner(x, distance):
        return lax.ppermute(x, "leaf", [(i, i ^ distance) for i in range(count)])

    first = from_partner(sums, 1)
    second = from_partner(sums + first, 2)
    return first, second, from_partner(sums + first + second, 4)


def shards(
    points,
    vectors,
    near_offset,
    leaf_basis,
    leaf_transfer,
    far_target,
    far_source,
    far_coupling,
    upper_transfer,
    upper_coupling,
):
    leaves, leaf_size, _ = leaf_basis.shape
    peers = lax.axis_size("top")
    region, peer = lax.axis_index("leaf"), lax.axis_index("top")
    place = region.astype(jnp.int32).reshape(1)
    first = ((region * peers + peer) * leaves).astype(jnp.int32).reshape(1)

    coefs = coefficients(place, vectors, leaf_basis, leaf_transfer, upper_transfer)
    gathered = lax.all_gather(coefs, "top", axis=0)
    before, after = neighbours(points, vectors, HALO * leaf_size)
    inputs = (first, near_offset.T, points, vectors, *before, *after)
    early_blocks = 2 * leaves
    early = near_field(inputs, early_blocks)
    gathered, early = lax.optimization_barrier((gathered, early))
    levels = siblings(jnp.sum(gathered[:, leaves:], axis=0))
    return last_field(
        inputs,
        early_blocks,
        early,
        place,
        far_target[0].T,
        far_source[0].T,
        levels,
        gathered,
        far_coupling[0],
        leaf_transfer,
        leaf_basis,
        upper_transfer,
        upper_coupling,
    )


def solution(mesh):
    split = ("leaf", "top")
    in_specs = (
        P(None, split),
        P(None, split),
        P(split, None),
        P(split, None, None),
        P(split, None, None),
        P(split, None, None),
        P(split, None, None),
        P(split, None, None, None, None),
        P(),
        P(),
    )
    return jax.shard_map(shards, mesh=mesh, in_specs=in_specs, out_specs=P(None, split), check_vma=False)
```

```python
import functools
import math

import jax
import jax.numpy as jnp
from jax import lax
from jax.experimental import pallas as pl
from jax.experimental.pallas import tpu as pltpu
from jax.sharding import PartitionSpec as P

F32, BF16 = jnp.float32, jnp.bfloat16
NUGGET = 0.1
SCALES = (0.3, 0.15, 0.15)
LOG2E = math.log2(math.e)
FACTOR = tuple(math.sqrt(3.0) * LOG2E / scale for scale in SCALES)
GAIN = -0.25 * math.log(2.0) * math.e
TINY = 1e-20
DEPTH = 64
HALO = 2
CHUNK = 64
UNROLL = 4
NEAR_LIMIT = 20 << 20
WIDE_LIMIT = 56 << 20
LAST_LIMIT = 56 << 20


def halves(x):
    high = x.astype(BF16)
    return high, (x - high.astype(F32)).astype(BF16)


def thirds(x):
    high = x.astype(BF16).astype(F32)
    rest = x - high
    middle = rest.astype(BF16).astype(F32)
    return high, middle, rest - middle


def dot_plain(x, matrix):
    n = matrix.shape[1]
    left = jnp.concatenate(halves(x), axis=0)
    out = jnp.dot(left, jnp.concatenate(halves(matrix), axis=1), preferred_element_type=F32)
    return out[0:8, 0:n] + out[8:16, 0:n] + out[0:8, n : 2 * n]


def dot_turned(x, matrix):
    high, low = halves(x)
    upper = jnp.concatenate([high, high], axis=1)
    lower = jnp.concatenate([low, jnp.zeros_like(low)], axis=1)
    out = lax.dot_general(
        jnp.concatenate([upper, lower], axis=0),
        jnp.concatenate(halves(matrix), axis=1),
        (((1,), (1,)), ((), ())),
        preferred_element_type=F32,
    )
    return out[0:8] + out[8:16]


def coef_kernel(place_ref, vec_hbm, basis_hbm, transfer_hbm, up0_ref, up1_ref, coef_ref, vec, basis, transfer, sems, *, group):
    del place_ref
    leaves, leaf_size, _ = basis.shape
    groups = leaves // group

    def copies(i):
        at = pl.ds(i * group, group)
        points = pl.ds(pl.multiple_of(i * (group * leaf_size), group * leaf_size), group * leaf_size)
        return (
            pltpu.make_async_copy(vec_hbm.at[:, points], vec.at[:, points], sems.at[0, i]),
            pltpu.make_async_copy(basis_hbm.at[at], basis.at[at], sems.at[1, i]),
            pltpu.make_async_copy(transfer_hbm.at[at], transfer.at[at], sems.at[2, i]),
        )

    for i in range(groups):
        for copy in copies(i):
            copy.start()

    def turn(i, total):
        for copy in copies(i):
            copy.wait()
        coefs = []
        for j in range(group):
            at = pl.ds(pl.multiple_of((i * group + j) * leaf_size, leaf_size), leaf_size)
            coefs.append(dot_plain(vec[:, at], basis[i * group + j]))
        for j in range(group):
            coef_ref[i * group + j] = coefs[j]
            total += dot_plain(coefs[j], transfer[i * group + j])
        return total

    part = lax.fori_loop(0, groups, turn, jnp.zeros(coef_ref.shape[1:], F32))
    coef_ref[leaves] = part
    part = dot_plain(part, up0_ref[0])
    coef_ref[leaves + 1] = part
    coef_ref[leaves + 2] = dot_plain(part, up1_ref[0])


def coefficients(place, vectors, leaf_basis, leaf_transfer, upper_transfer):
    leaves, leaf_size, rank = leaf_basis.shape
    columns = vectors.shape[0]
    group = 4
    node = (1, rank, rank)
    hbm = pl.BlockSpec(memory_space=pl.ANY)
    return pl.pallas_call(
        functools.partial(coef_kernel, group=group),
        grid_spec=pltpu.PrefetchScalarGridSpec(
            num_scalar_prefetch=1,
            grid=(1,),
            in_specs=[
                hbm,
                hbm,
                hbm,
                pl.BlockSpec(node, lambda i, p: (p[0], 0, 0)),
                pl.BlockSpec(node, lambda i, p: (8 + (p[0] >> 1), 0, 0)),
            ],
            out_specs=pl.BlockSpec((leaves + 3, columns, rank), lambda i, p: (0, 0, 0)),
            scratch_shapes=[
                pltpu.VMEM(vectors.shape, F32),
                pltpu.VMEM(leaf_basis.shape, F32),
                pltpu.VMEM(leaf_transfer.shape, F32),
                pltpu.SemaphoreType.DMA((3, leaves // group)),
            ],
        ),
        out_shape=jax.ShapeDtypeStruct((leaves + 3, columns, rank), F32),
        compiler_params=pltpu.CompilerParams(vmem_limit_bytes=WIDE_LIMIT),
        cost_estimate=pl.CostEstimate(
            flops=leaves * 16 * rank * (leaf_size + rank) * 4,
            bytes_accessed=4 * leaves * rank * (leaf_size + rank),
            transcendentals=0,
        ),
    )(place, vectors, leaf_basis, leaf_transfer, upper_transfer, upper_transfer)


def features(x, target):
    row = lax.broadcasted_iota(jnp.int32, x.shape, 0)
    norm = jnp.sum(x * x, axis=0, keepdims=True)
    if target:
        high, middle, low = thirds(jnp.where(row < 3, -2.0 * x, norm))
        groups = [jnp.where(row == 3, 1.0, high), jnp.where(row == 3, 1.0, middle)]
        groups += [jnp.where(row == 3, 1.0, jnp.where(row < 3, high, low)), low, middle, high]
    else:
        high, middle, low = thirds(jnp.where(row < 4, jnp.where(row < 3, x, norm), 0.0))
        one = jnp.where(row == 4, 1.0, 0.0)
        groups = [high + one, middle + one, low + one]
        groups += [jnp.where(row < 3, high, 0.0), jnp.where(row < 3, high, 0.0), jnp.where(row < 3, middle, 0.0)]
    groups += [jnp.zeros_like(x)] * (DEPTH // 8 - 6)
    return jnp.concatenate(groups, axis=0)


def matern(dist_sq):
    nt = -LOG2E - dist_sq * lax.rsqrt(dist_sq)
    return nt * jnp.exp2(nt)


def near_core(inputs, out_ref, scratch, *, begin, stop, leaf_size):
    first_ref, offset_ref, points_ref, vectors_ref, before_p, before_v, after_p, after_v = inputs
    wide_scr, x_scr, a_scr, v_scr, b0, b1, u_scr, kh_scr, kl_scr, item_g, item_h = scratch
    slots, leaves = offset_ref.shape
    first = first_ref[0]
    row8 = lax.broadcasted_iota(jnp.int32, (8, leaf_size), 0)

    wide_scr[...] = jnp.zeros_like(wide_scr)

    def listing(g, n):
        item_g[n] = g
        item_h[n] = g + HALO
        n = n + 1
        for j in range(slots):
            offset = offset_ref[j, g]
            item_g[n] = g
            item_h[n] = g + HALO + offset
            n = n + jnp.where(offset != 0, 1, 0)
        return n

    count = lax.fori_loop(0, leaves, listing, 0)
    end = count if stop is None else jnp.minimum(stop, count)
    g_first = item_g[jnp.minimum(begin, count - 1)]
    g_last = item_g[end - 1]

    def prepare(p_ref, v_ref, start, stop, origin):
        def turn(h, _):
            at = pl.ds(pl.multiple_of((h - origin) * leaf_size, leaf_size), leaf_size)
            to = h + HALO
            centre = (first + h).astype(F32) * 0.5 + 0.5
            wide_scr[0:3] = p_ref[:, at]
            shift = jnp.where(row8 == 0, centre, 0.5)
            scale = jnp.where(row8 == 0, FACTOR[0], FACTOR[1])
            x = jnp.where(row8 < 3, (wide_scr[...] - shift) * scale, 0.0)
            x_scr[to] = x
            a_scr[to] = features(x, False).T.astype(BF16)
            v_high, v_low = halves(v_ref[:, at])
            v_scr[to, 0:16] = jnp.concatenate([v_high, v_low], axis=0)
            v_scr[to, 16:32] = jnp.concatenate([v_high, jnp.zeros_like(v_high)], axis=0)
            return 0

        lax.fori_loop(start, stop, turn, 0)

    prepare(before_p, before_v, jnp.minimum(g_first - HALO, 0), 0, -HALO)
    prepare(points_ref, vectors_ref, jnp.maximum(g_first - HALO, 0), jnp.minimum(g_last + HALO + 1, leaves), 0)
    prepare(after_p, after_v, leaves, jnp.maximum(g_last + HALO + 1, leaves), leaves)

    def target_features(i, b_scr):
        i = jnp.minimum(i, count - 1)
        g, h = item_g[i], item_h[i]
        apart = (g + HALO - h).astype(F32) * (0.5 * FACTOR[0])
        x = x_scr[g + HALO]
        b_scr[...] = features(jnp.where(row8 == 0, x + apart, x), True).astype(BF16)

    def distances(i, b_scr, c, size):
        h = item_h[jnp.minimum(i, count - 1)]
        dist_sq = jnp.dot(a_scr[h, c : c + size], b_scr[...], preferred_element_type=F32)
        u_scr[c : c + size] = jnp.maximum(dist_sq, TINY)

    def turn(i, b_next, b_later):
        now = jnp.minimum(i, count - 1)
        h = item_h[now]
        acc = jnp.zeros((16, leaf_size), F32)
        size = CHUNK
        for c in range(0, leaf_size, size):
            for r in range(c, c + size, 32):
                high, low = halves(matern(u_scr[r : r + 32]))
                kh_scr[r : r + 32] = high
                kl_scr[r : r + 32] = low
            distances(i + 1, b_next, c, size)
            acc += jnp.dot(v_scr[h, 0:16, c : c + size], kh_scr[c : c + size], preferred_element_type=F32)
            acc += jnp.dot(v_scr[h, 16:32, c : c + size], kl_scr[c : c + size], preferred_element_type=F32)
        target_features(i + 2, b_later)
        done = jnp.where(i < end, (acc[0:8] + acc[8:16]) * GAIN, 0.0)
        at = pl.ds(pl.multiple_of(item_g[now] * leaf_size, leaf_size), leaf_size)
        out_ref[:, at] += done

    target_features(begin, b0)
    target_features(begin + 1, b1)
    distances(begin, b0, 0, leaf_size)

    def turns(i, _):
        for j in range(0, UNROLL, 2):
            turn(begin + UNROLL * i + j, b1, b0)
            turn(begin + UNROLL * i + j + 1, b0, b1)
        return 0

    lax.fori_loop(0, jnp.maximum(end - begin + (UNROLL - 1), 0) >> UNROLL.bit_length() - 1, turns, 0)


def near_scratch(count, slots, leaf_size):
    square = (leaf_size, leaf_size)
    leaves = count + 2 * HALO
    return [
        pltpu.VMEM((8, leaf_size), F32),
        pltpu.VMEM((leaves, 8, leaf_size), F32),
        pltpu.VMEM((leaves, leaf_size, DEPTH), BF16),
        pltpu.VMEM((leaves, 32, leaf_size), BF16),
        pltpu.VMEM((DEPTH, leaf_size), BF16),
        pltpu.VMEM((DEPTH, leaf_size), BF16),
        pltpu.VMEM(square, F32),
        pltpu.VMEM(square, BF16),
        pltpu.VMEM(square, BF16),
        pltpu.SMEM((count * (slots + 1) + 8,), jnp.int32),
        pltpu.SMEM((count * (slots + 1) + 8,), jnp.int32),
    ]


NEAR_INPUTS = 8


def near_kernel(*refs, stop, leaf_size):
    inputs, out_ref = refs[:NEAR_INPUTS], refs[NEAR_INPUTS]
    out_ref[...] = NUGGET * inputs[3][...]
    near_core(inputs, out_ref, refs[NEAR_INPUTS + 1 :], begin=0, stop=stop, leaf_size=leaf_size)


def near_cost(blocks, leaves, leaf_size):
    return pl.CostEstimate(
        flops=blocks * leaf_size * leaf_size * 512,
        bytes_accessed=8 * 11 * leaves * leaf_size,
        transcendentals=blocks * 2 * leaf_size * leaf_size,
    )


def near_specs():
    return [pl.BlockSpec(memory_space=pltpu.SMEM)] * 2 + [pl.BlockSpec(memory_space=pltpu.VMEM)] * 6


def near_field(inputs, stop):
    slots, leaves = inputs[1].shape
    columns, points = inputs[3].shape
    leaf_size = points // leaves
    return pl.pallas_call(
        functools.partial(near_kernel, stop=stop, leaf_size=leaf_size),
        in_specs=near_specs(),
        out_specs=pl.BlockSpec(memory_space=pltpu.VMEM),
        out_shape=jax.ShapeDtypeStruct((columns, points), F32),
        scratch_shapes=near_scratch(leaves, slots, leaf_size),
        compiler_params=pltpu.CompilerParams(vmem_limit_bytes=NEAR_LIMIT),
        cost_estimate=near_cost(stop, leaves, leaf_size),
    )(*inputs)


def last_kernel(*refs, begin, leaf_size):
    inputs = refs[:NEAR_INPUTS]
    done_ref, place_ref, target_ref, source_ref, level0, level1, level2, *hbm, out_ref = refs[NEAR_INPUTS : NEAR_INPUTS + 14]
    coef, coupling, transfer, basis, down, across, local_scr, sems, *scratch = refs[NEAR_INPUTS + 14 :]
    held = (coef, coupling, transfer, basis, down, across)
    peers, slots, _, _ = coupling.shape
    leaves = basis.shape[0]
    parts = sems.shape[1]

    def copies():
        for i, (source, target) in enumerate(zip(hbm, held, strict=True)):
            number = math.gcd(parts, source.shape[0])
            size = source.shape[0] // number
            for j in range(number):
                at = pl.ds(j * size, size)
                yield pltpu.make_async_copy(source.at[at], target.at[at], sems.at[i, j])

    for copy in copies():
        copy.start()

    out_ref[...] = done_ref[...]
    local_scr[...] = jnp.zeros_like(local_scr)
    near_core(inputs, out_ref, scratch, begin=begin, stop=None, leaf_size=leaf_size)

    for copy in copies():
        copy.wait()

    here = place_ref[0]
    region = dot_plain(level2[2], across[12 + (here >> 2)])
    region = dot_plain(level1[1], across[8 + (here >> 1)]) + dot_turned(region, down[8 + (here >> 1)])
    region = dot_plain(level0[0], across[here]) + dot_turned(region, down[here])

    def far(p, _):
        products = [dot_plain(coef[p, source_ref[k, p]], coupling[p, k]) for k in range(slots)]
        for k in range(slots):
            local_scr[target_ref[k, p]] += products[k]
        return 0

    lax.fori_loop(0, peers, far, 0, unroll=4)

    group = 8

    def back(i, _):
        locals_ = [local_scr[i * group + j] + dot_turned(region, transfer[i * group + j]) for j in range(group)]
        for j in range(group):
            at = pl.ds(pl.multiple_of((i * group + j) * leaf_size, leaf_size), leaf_size)
            out_ref[:, at] += dot_turned(locals_[j], basis[i * group + j])
        return 0

    lax.fori_loop(0, leaves // group, back, 0)


def last_field(inputs, begin, done, place, targets, sources, levels, coefs, far_coupling, leaf_transfer, leaf_basis, upper_transfer, upper_coupling):
    leaves, leaf_size, rank = leaf_basis.shape
    columns, points = inputs[3].shape
    slots = inputs[1].shape[0]
    smem, vmem = pl.BlockSpec(memory_space=pltpu.SMEM), pl.BlockSpec(memory_space=pltpu.VMEM)
    hbm = pl.BlockSpec(memory_space=pl.ANY)
    streamed = (coefs, far_coupling, leaf_transfer, leaf_basis, upper_transfer, upper_coupling)
    return pl.pallas_call(
        functools.partial(last_kernel, begin=begin, leaf_size=leaf_size),
        in_specs=near_specs() + [vmem, smem, smem, smem, vmem, vmem, vmem] + [hbm] * len(streamed),
        out_specs=vmem,
        out_shape=jax.ShapeDtypeStruct((columns, points), F32),
        scratch_shapes=[pltpu.VMEM(x.shape, F32) for x in streamed]
        + [pltpu.VMEM((leaves + 1, columns, rank), F32), pltpu.SemaphoreType.DMA((len(streamed), 8))]
        + near_scratch(leaves, slots, leaf_size),
        compiler_params=pltpu.CompilerParams(vmem_limit_bytes=LAST_LIMIT),
        cost_estimate=near_cost(leaves, leaves, leaf_size),
    )(*inputs, done, place, targets, sources, *levels, *streamed)


def neighbours(points, vectors, width):
    axes = ("leaf", "top")
    count = lax.axis_size("leaf") * lax.axis_size("top")
    head, tail = (jnp.concatenate([points[:, s], vectors[:, s]], axis=0) for s in (slice(0, width), slice(-width, None)))
    before = lax.ppermute(tail, axes, [(i, i + 1) for i in range(count - 1)])
    after = lax.ppermute(head, axes, [(i + 1, i) for i in range(count - 1)])
    return (before[:3], before[3:]), (after[:3], after[3:])


def siblings(sums):
    count = lax.axis_size("leaf")

    def from_partner(x, distance):
        return lax.ppermute(x, "leaf", [(i, i ^ distance) for i in range(count)])

    first = from_partner(sums, 1)
    second = from_partner(sums + first, 2)
    return first, second, from_partner(sums + first + second, 4)


def shards(
    points,
    vectors,
    near_offset,
    leaf_basis,
    leaf_transfer,
    far_target,
    far_source,
    far_coupling,
    upper_transfer,
    upper_coupling,
):
    leaves, leaf_size, _ = leaf_basis.shape
    peers = lax.axis_size("top")
    region, peer = lax.axis_index("leaf"), lax.axis_index("top")
    place = region.astype(jnp.int32).reshape(1)
    first = ((region * peers + peer) * leaves).astype(jnp.int32).reshape(1)

    coefs = coefficients(place, vectors, leaf_basis, leaf_transfer, upper_transfer)
    gathered = lax.all_gather(coefs, "top", axis=0)
    before, after = neighbours(points, vectors, HALO * leaf_size)
    inputs = (first, near_offset.T, points, vectors, *before, *after)
    early_blocks = 2 * leaves
    early = near_field(inputs, early_blocks)
    gathered, early = lax.optimization_barrier((gathered, early))
    levels = siblings(jnp.sum(gathered[:, leaves:], axis=0))
    return last_field(
        inputs,
        early_blocks,
        early,
        place,
        far_target[0].T,
        far_source[0].T,
        levels,
        gathered,
        far_coupling[0],
        leaf_transfer,
        leaf_basis,
        upper_transfer,
        upper_coupling,
    )


def solution(mesh):
    split = ("leaf", "top")
    in_specs = (
        P(None, split),
        P(None, split),
        P(split, None),
        P(split, None, None),
        P(split, None, None),
        P(split, None, None),
        P(split, None, None),
        P(split, None, None, None, None),
        P(),
        P(),
    )
    return jax.shard_map(shards, mesh=mesh, in_specs=in_specs, out_specs=P(None, split), check_vma=False)
```
